32 devices in a mesh: ctx: 16 (over z, x, core), head: 2 (over y).
Axes of the slice: x: 2, y: 2, z: 4, core: 2. Of those that a mesh axis runs over, the one named last changes fastest.
Arguments:
- x_in: bfloat16 [4096, 5120], P('ctx', 'head'), may hold values from -6 to 6
- z_in: bfloat16 [4096, 5120], P('ctx', 'head'), may hold values from -48 to 48
- bc_in: bfloat16 [256, 4096], P('head', 'ctx'), may hold values from -6 to 6
- dt_in: float32 [80, 4096], P('head', 'ctx'), may hold values from -1 to 1
- dt_bias: float32 [80], P('head'), may hold values from -6 to 1
- decay_rate: float32 [80], P('head'), may hold values from 0 to 1, as said below
- d_skip: float32 [80], P('head'), may hold values from 1 to 6
- conv_x: float32 [4, 5120], P(None, 'head'), may hold values from -3 to 3
- conv_bc: float32 [256, 4], replicated, may hold values from -3 to 3
- norm_gain: float32 [5120], P('head'), may hold values from 0.1 to 1.9
- w_out: bfloat16 [5120, 2560], P('head'), may hold values from -0.125 to 0.125
Outputs:
- layer_out: bfloat16 [2560, 4096], P('head', 'ctx')
The draws below stay inside these ranges and needn't reach their ends.
Inputs may be any that keep to these rules, and one draw needn't show every extreme that they name: `decay_rate`: each head's decay rate is positive.
All inputs are finite; a program needn't handle non-finite values.
Results may differ from the reference program's by a relative error of at most 0.019.
Values may be sent and summed in bfloat16 or wider, within the bound.
A program may use at most 128 MiB of HBM per device.

```python
import math
import jax
import jax.numpy as jnp
from jax import lax

D = 2560
HEADS = 80
N = 128
P_SIZE = 64
KCONV = 4
SPAN = 256
TOKENS = 4096
N_HEAD = 2


def rates_and_bias(key):
    base_key = jax.random.fold_in(key, 11)
    key_pick, key_fast, key_slow, key_bias = jax.random.split(base_key, 4)
    fast_share = 0.5
    quick_head = jax.random.uniform(key_pick, (HEADS,)) < fast_share
    fast_rate = jnp.exp(jax.random.uniform(key_fast, (HEADS,), minval=math.log(1.0 / 50.0), maxval=math.log(1.0 / 30.0)))
    slow_rate = jnp.exp(jax.random.uniform(key_slow, (HEADS,), minval=math.log(30.0), maxval=math.log(100.0))) / TOKENS
    bias_draw = jax.random.uniform(key_bias, (HEADS,), minval=-6.0, maxval=-4.0)
    head_rate = jnp.where(quick_head, fast_rate, jnp.minimum(slow_rate, 0.5))
    head_bias = jnp.where(quick_head, bias_draw + 5.0, bias_draw)
    return (head_rate.astype(jnp.float32), head_bias.astype(jnp.float32))


def draw_decay_rate(key, part):
    head_rate, head_bias = rates_and_bias(key)
    return head_rate


def draw_dt_bias(key, part):
    head_rate, head_bias = rates_and_bias(key)
    return head_bias


def draw_z_in(key, part):
    key_base, key_cols, key_rows = jax.random.split(key, 3)
    col_total = HEADS * P_SIZE
    base_vals = jnp.clip(jax.random.normal(key_base, (TOKENS, col_total), jnp.float32), -4.0, 4.0)
    ramp_pos = jnp.arange(col_total, dtype=jnp.float32) / col_total
    col_scale = jnp.exp(0.5 * math.log(3.0) * ramp_pos) * jnp.exp(jax.random.uniform(key_cols, (col_total,), minval=-0.7, maxval=0.7))
    row_scale = jnp.exp(jax.random.uniform(key_rows, (TOKENS, 1), minval=math.log(0.5), maxval=math.log(2.0)))
    return (base_vals * col_scale[None, :] * row_scale).astype(jnp.bfloat16)


def raised(drawn, rng, source, target, parts, factor):
    owner, partner = [(jnp.arange(drawn.shape[dim]) // (drawn.shape[dim] // parts)).reshape([-1 if axis == dim else 1 for axis in range(drawn.ndim)]) for dim in (source, target)]
    chosen = jax.random.permutation(rng, parts)[partner]
    strong = (owner == chosen) | (owner == (partner + parts // 2) % parts)
    return jnp.where(strong, factor * drawn, drawn)


def level_of(key, dims, shards, smallest, largest):
    level, own = 1.0, jax.random.fold_in(key, 6)
    for position, parts in shards:
        steps = jnp.exp(jax.random.uniform(jax.random.fold_in(own, position), (parts,), jnp.float32, smallest / len(shards), largest / len(shards)))
        level = level * jnp.repeat(steps, dims[position] // parts).reshape([-1 if axis == position else 1 for axis in range(len(dims))])
    return level


def bell_draw(own_key, extent, scale, most, cuts=(), held_as=jnp.bfloat16):
    result = scale * jax.random.normal(own_key, extent, jnp.float32)
    if cuts:
        result = result * level_of(own_key, extent, cuts, -0.22, 0.18)
    return jnp.clip(result, -most, most).astype(held_as)


def noise_with(own_key, shape, deviation, reach, shards, heavy, kind=jnp.bfloat16):
    array = deviation * jax.random.normal(own_key, shape, jnp.float32)
    if shards:
        array = array * level_of(own_key, shape, shards, -0.22, 0.18)
    return jnp.clip(raised(array, jax.random.fold_in(own_key, 3), *heavy), -reach, reach).astype(kind)


def setup_inputs(seed: int = 0) -> dict:
    streams_of = jax.random.split(jax.random.key(seed), 12)
    x_in = bell_draw(streams_of[0], (TOKENS, HEADS * P_SIZE), 1.0, 6.0, ((0, 16), (1, 2)))
    z_in = draw_z_in(jax.random.fold_in(streams_of[11], 71), 0)
    bc_in = bell_draw(streams_of[2], (2 * N, TOKENS), 1.0, 6.0, ((0, 2), (1, 16)))
    dt_in = jnp.clip(jax.random.uniform(streams_of[3], (HEADS, TOKENS), jnp.float32, -1.0, 1.0) * level_of(streams_of[3], (HEADS, TOKENS), ((0, 2), (1, 16)), -0.4, 0.0), -1.0, 1.0)
    dt_bias = draw_dt_bias(jax.random.fold_in(streams_of[11], 71), 0)
    decay_rate = draw_decay_rate(jax.random.fold_in(streams_of[11], 71), 0)
    d_skip = jnp.clip(1.0 + 5.0 * jax.random.uniform(streams_of[6], (HEADS,), jnp.float32) ** level_of(streams_of[6], (HEADS,), ((0, 2),), -0.2, 0.2), 1.0, 6.0)
    conv_x = bell_draw(streams_of[7], (KCONV, HEADS * P_SIZE), KCONV ** -0.5, 3.0, ((1, 2),), jnp.float32)
    conv_bc = bell_draw(streams_of[8], (2 * N, KCONV), KCONV ** -0.5, 3.0, (), jnp.float32)
    norm_gain = jnp.clip(1.0 + 0.18 * jax.random.normal(streams_of[9], (HEADS * P_SIZE,), jnp.float32), 0.1, 1.9)
    w_out = noise_with(streams_of[10], (HEADS * P_SIZE, D), (HEADS * P_SIZE) ** -0.5, 0.125, ((0, 2),), (0, 1, 2, 2.0))
    return {"x_in": x_in, "z_in": z_in, "bc_in": bc_in, "dt_in": dt_in, "dt_bias": dt_bias, "decay_rate": decay_rate, "d_skip": d_skip, "conv_x": conv_x, "conv_bc": conv_bc, "norm_gain": norm_gain, "w_out": w_out}


EPSILON = 1e-05

def conv_rows(padded, taps, length):
    summed = jnp.zeros((length, padded.shape[1]), jnp.float32)
    for tap_index in range(taps.shape[0]):
        summed = summed + taps[tap_index][None, :] * padded[tap_index:tap_index + length].astype(jnp.float32)
    return summed

def conv_cols(padded, taps, length):
    summed = jnp.zeros((padded.shape[0], length), jnp.float32)
    for tap_index in range(taps.shape[1]):
        summed = summed + taps[:, tap_index][:, None] * padded[:, tap_index:tap_index + length].astype(jnp.float32)
    return summed

def block_terms(x_block, b_block, c_block, dt_block, step_block):
    cum_log = jnp.cumsum(step_block, axis=1)
    scores = lax.dot_general(c_block, b_block, (((0,), (0,)), ((), ())), preferred_element_type=jnp.float32)
    length = cum_log.shape[1]
    row_ids = lax.broadcasted_iota(jnp.int32, (length, length), 0)
    col_ids = lax.broadcasted_iota(jnp.int32, (length, length), 1)
    lower_mask = row_ids >= col_ids
    log_gap = jnp.where(lower_mask[None], cum_log[:, :, None] - cum_log[:, None, :], -jnp.inf)
    weights = (scores[None] * jnp.exp(log_gap) * dt_block[:, None, :]).astype(jnp.bfloat16)
    local_y = jnp.einsum('hts,shp->thp', weights.astype(jnp.float32), x_block.astype(jnp.float32))
    tail_scale = jnp.exp(cum_log[:, -1:] - cum_log) * dt_block
    scaled = (x_block.astype(jnp.float32) * tail_scale.T[:, :, None]).astype(jnp.bfloat16)
    states = jnp.einsum('shp,ns->hpn', scaled.astype(jnp.float32), b_block.astype(jnp.float32))
    return (cum_log, local_y, states)

def reference(x_in, z_in, bc_in, dt_in, dt_bias, decay_rate, d_skip, conv_x, conv_bc, norm_gain, w_out):
    rim_rows = conv_x.shape[0] - 1
    length = x_in.shape[0]
    x_pad = jnp.concatenate([jnp.zeros((rim_rows, x_in.shape[1]), x_in.dtype), x_in], 0)
    xconv = jax.nn.silu(conv_rows(x_pad, conv_x, length)).astype(jnp.bfloat16)
    bc_pad = jnp.concatenate([jnp.zeros((bc_in.shape[0], rim_rows), bc_in.dtype), bc_in], 1)
    bcconv = jax.nn.silu(conv_cols(bc_pad, conv_bc, length)).astype(jnp.bfloat16)
    delta_t = jax.nn.softplus(dt_in + dt_bias[:, None])
    log_step = -delta_t * decay_rate[:, None]
    blocks = length // SPAN
    x_blocks = xconv.reshape(blocks, SPAN, HEADS, P_SIZE)
    b_blocks = bcconv[:N].reshape(N, blocks, SPAN).transpose(1, 0, 2)
    c_blocks = bcconv[N:].reshape(N, blocks, SPAN).transpose(1, 0, 2)
    dt_blocks = delta_t.reshape(HEADS, blocks, SPAN).transpose(1, 0, 2)
    step_blocks = log_step.reshape(HEADS, blocks, SPAN).transpose(1, 0, 2)
    z_blocks = z_in.reshape(blocks, SPAN, HEADS * P_SIZE)

    def advance(carry_state, block_item):
        x_block, b_block, c_block, dt_block, step_block, z_block = block_item
        cum_log, local_y, states = block_terms(x_block, b_block, c_block, dt_block, step_block)
        carried = jnp.einsum('nt,hpn->thp', c_block.astype(jnp.float32), carry_state, precision=lax.Precision.HIGHEST) * jnp.exp(cum_log).T[:, :, None]
        y_total = local_y + carried + d_skip[None, :, None] * x_block.astype(jnp.float32)
        gated_y = y_total.reshape(SPAN, HEADS * P_SIZE) * jax.nn.silu(z_block.astype(jnp.float32))
        mean_sq = lax.optimization_barrier(jnp.sum(gated_y * gated_y, axis=1, keepdims=True)) / (HEADS * P_SIZE)
        hidden = (gated_y * lax.rsqrt(mean_sq + EPSILON) * norm_gain[None, :]).astype(jnp.bfloat16)
        carry_state = jnp.exp(cum_log[:, -1])[:, None, None] * carry_state + states
        return (carry_state, hidden)
    start_state = jnp.zeros((HEADS, P_SIZE, N), jnp.float32)
    _, hidden = lax.scan(advance, start_state, (x_blocks, b_blocks, c_blocks, dt_blocks, step_blocks, z_blocks))
    hidden = hidden.reshape(length, HEADS * P_SIZE)
    group_cols = HEADS * P_SIZE // N_HEAD
    summed = jnp.zeros((length, w_out.shape[1]), jnp.float32)
    for group_index in range(N_HEAD):
        lo_col = group_index * group_cols
        partial_value = jnp.dot(hidden[:, lo_col:lo_col + group_cols], w_out[lo_col:lo_col + group_cols], preferred_element_type=jnp.float32).astype(jnp.bfloat16)
        partial_value = lax.optimization_barrier(partial_value)
        summed = summed + partial_value.astype(jnp.float32)
    return summed.astype(jnp.bfloat16).T
```

```python
import functools

import jax
import jax.numpy as jnp
from jax import lax
from jax.experimental import pallas as pl
from jax.experimental.pallas import tpu as pltpu
from jax.sharding import PartitionSpec as P

HEADS = 80
N = 128
P_SIZE = 64
KCONV = 4
SPAN = 256


EPSILON = 1e-05
MESH = pl.DeviceIdType.MESH


def from_behind(value, axis, steps):
    count = lax.axis_size(axis)
    first, last = (max(0, -steps), min(count, count - steps))
    return lax.ppermute(value, axis, [(source, source + steps) for source in range(first, last)])


def scan_kernel(
    groups, parts, s_ref, k_ref, e_ref,
    ra, rka, tb, ktb, rb, rkb, sc, rc, sd, rd, oe, se, send, recv, ksend, krecv,
):
    idx = lax.axis_index("ctx")
    hd = lax.axis_index("head")
    c = lax.rem(idx, 2)
    x = lax.rem(lax.div(idx, 2), 2)
    g = lax.div(idx, 4)
    core_peer = idx + 1 - 2 * c
    x_peer = idx + 2 - 4 * x
    has_prev = g > 0
    has_next = g < groups - 1
    heads = k_ref.shape[0]
    size = heads // parts

    barrier = pltpu.get_barrier_semaphore()
    pl.semaphore_signal(barrier, inc=1, device_id=(core_peer, hd), device_id_type=MESH)
    pl.semaphore_signal(barrier, inc=1, device_id=(x_peer, hd), device_id_type=MESH)

    @pl.when(has_prev)
    def _():
        pl.semaphore_signal(barrier, inc=1, device_id=(idx - 4, hd), device_id_type=MESH)

    @pl.when(has_next)
    def _():
        pl.semaphore_signal(barrier, inc=1, device_id=(idx + 4, hd), device_id_type=MESH)

    pl.semaphore_wait(barrier, 2 + has_prev.astype(jnp.int32) + has_next.astype(jnp.int32))

    def copy(src, dst, phase, j, dev):
        return pltpu.make_async_remote_copy(
            src_ref=src, dst_ref=dst, send_sem=send.at[phase, j], recv_sem=recv.at[phase, j],
            device_id=(dev, hd), device_id_type=MESH,
        )

    def keep_copy(src, dst, j, dev):
        return pltpu.make_async_remote_copy(
            src_ref=src, dst_ref=dst, send_sem=ksend.at[j], recv_sem=krecv.at[j],
            device_id=(dev, hd), device_id_type=MESH,
        )

    part = [pl.ds(j * size, size) for j in range(parts)]
    f32, bf16 = jnp.float32, jnp.bfloat16
    ka = keep_copy(k_ref, rka, 0, core_peer)
    ka.start()
    step_a = [copy(s_ref.at[1 - c, :, d], ra.at[:, d], 0, j, core_peer) for j, d in enumerate(part)]
    for cp in step_a:
        cp.start()

    @pl.when(jnp.logical_not(has_prev))
    def _():
        rc[...] = jnp.zeros_like(rc)

    ka.wait_recv()
    ktb[...] = k_ref[...] * rka[...]
    kb = keep_copy(ktb, rkb, 1, x_peer)
    kb.start()
    is_core0 = c == 0
    is_x0 = x == 0

    step_b = [copy(tb.at[1 - x, d], rb.at[d], 1, j, x_peer) for j, d in enumerate(part)]
    for j, d in enumerate(part):
        step_a[j].wait_recv()
        own = s_ref[c, :, d].astype(f32)
        peer = ra[:, d].astype(f32)
        first = jnp.where(is_core0, own, peer)
        second = jnp.where(is_core0, peer, own)
        keep = jnp.where(is_core0, rka[d], k_ref[d])
        tb[:, d] = (keep[None, :, None, :] * first + second).astype(bf16)
        step_b[j].start()

    kb.wait_recv()
    step_c = [copy(sc.at[d], rc.at[d], 2, j, idx + 4) for j, d in enumerate(part)]
    step_d = [copy(sd.at[d], rd.at[d], 3, j, x_peer) for j, d in enumerate(part)]
    for j, d in enumerate(part):
        step_b[j].wait_recv()
        own = tb[x, d].astype(f32)
        peer = rb[d].astype(f32)
        first = jnp.where(is_x0, own, peer)
        second = jnp.where(is_x0, peer, own)
        keep0 = jnp.where(is_x0, ktb[d], rkb[d])[:, None, :]
        keep1 = jnp.where(is_x0, rkb[d], ktb[d])[:, None, :]

        @pl.when(has_prev)
        def _():
            step_c[j].wait_recv()

        entry = rc[d].astype(f32)
        after = keep0 * entry + first

        @pl.when(has_next)
        def _():
            sc[d] = (keep1 * after + second).astype(bf16)
            step_c[j].start()

        sd[d] = jnp.where(is_x0, after, entry).astype(bf16)
        step_d[j].start()
        oe[d] = jnp.where(is_x0, entry, after).astype(bf16)

    step_e = [copy(se.at[:, d], e_ref.at[c, :, d], 4, j, core_peer) for j, d in enumerate(part)]
    for j, d in enumerate(part):
        step_d[j].wait_recv()
        keep = jnp.where(is_core0, k_ref[d], rka[d])[:, None, :]
        for quarter, source in ((x, oe), (1 - x, rd)):
            entry = source[d].astype(f32)
            mine = jnp.where(is_core0, s_ref[c, quarter, d].astype(f32), ra[quarter, d].astype(f32))
            after = keep * entry + mine
            e_ref[c, quarter, d] = jnp.where(is_core0, entry, after).astype(bf16)
            se[quarter, d] = jnp.where(is_core0, after, entry).astype(bf16)
        step_e[j].start()

    for cp in step_e:
        cp.wait_recv()
    ka.wait_send()
    kb.wait_send()
    for j in range(parts):
        step_a[j].wait_send()
        step_b[j].wait_send()
        step_d[j].wait_send()
        step_e[j].wait_send()

    @pl.when(has_next)
    def _():
        for cp in step_c:
            cp.wait_send()


def entering_states(states, keep):
    heads = keep.shape[0]
    groups = lax.axis_size("ctx") // 4
    parts = 5
    quarter = (heads,) + states.shape[3:]
    vmem = pl.BlockSpec(memory_space=pltpu.VMEM)
    bf = jnp.bfloat16
    return pl.pallas_call(
        functools.partial(scan_kernel, groups, parts),
        out_shape=jax.ShapeDtypeStruct(states.shape, bf),
        in_specs=[vmem, vmem],
        out_specs=vmem,
        scratch_shapes=[
            pltpu.VMEM((2,) + quarter, bf),
            pltpu.VMEM(keep.shape, jnp.float32),
            pltpu.VMEM((2,) + quarter, bf),
            pltpu.VMEM(keep.shape, jnp.float32),
            pltpu.VMEM(quarter, bf),
            pltpu.VMEM(keep.shape, jnp.float32),
            pltpu.VMEM(quarter, bf),
            pltpu.VMEM(quarter, bf),
            pltpu.VMEM(quarter, bf),
            pltpu.VMEM(quarter, bf),
            pltpu.VMEM(quarter, bf),
            pltpu.VMEM((2,) + quarter, bf),
            pltpu.SemaphoreType.DMA((5, parts)),
            pltpu.SemaphoreType.DMA((5, parts)),
            pltpu.SemaphoreType.DMA((2,)),
            pltpu.SemaphoreType.DMA((2,)),
        ],
        compiler_params=pltpu.CompilerParams(
            collective_id=0, has_side_effects=True, vmem_limit_bytes=32 * 1024 * 1024
        ),
    )(states, keep)


def conv_rows(padded, taps, length):
    summed = jnp.zeros((length, padded.shape[1]), jnp.float32)
    for tap_index in range(taps.shape[0]):
        summed = summed + taps[tap_index][None, :] * padded[tap_index : tap_index + length].astype(
            jnp.float32
        )
    return summed


def conv_cols(padded, taps, length):
    summed = jnp.zeros((padded.shape[0], length), jnp.float32)
    for tap_index in range(taps.shape[1]):
        summed = summed + taps[:, tap_index][:, None] * padded[
            :, tap_index : tap_index + length
        ].astype(jnp.float32)
    return summed


def block_local(x_block, b_block, c_block, dt_block, step_block):
    cum_log = jnp.cumsum(step_block, axis=1)
    scores = lax.dot_general(
        c_block, b_block, (((0,), (0,)), ((), ())), preferred_element_type=jnp.float32
    )
    length = cum_log.shape[1]
    row_ids = lax.broadcasted_iota(jnp.int32, (length, length), 0)
    col_ids = lax.broadcasted_iota(jnp.int32, (length, length), 1)
    lower_mask = row_ids >= col_ids
    log_gap = jnp.where(lower_mask[None], cum_log[:, :, None] - cum_log[:, None, :], -jnp.inf)
    weights = (scores[None] * jnp.exp(log_gap) * dt_block[:, None, :]).astype(jnp.bfloat16)
    local_y = jnp.einsum("hts,shp->thp", weights, x_block, preferred_element_type=jnp.float32)
    tail_scale = jnp.exp(cum_log[:, -1:] - cum_log) * dt_block
    scaled = (x_block.astype(jnp.float32) * tail_scale.T[:, :, None]).astype(jnp.bfloat16)
    states = jnp.einsum("shp,ns->hpn", scaled, b_block, preferred_element_type=jnp.float32)
    return (cum_log, local_y, states)


def on_device(
    x_in, z_in, bc_in, dt_in, dt_bias, decay_rate, d_skip, conv_x, conv_bc, norm_gain, w_out
):
    tok_rows = x_in.shape[0]
    hid_cols = x_in.shape[1]
    head_count = hid_cols // P_SIZE
    rim_rows = KCONV - 1
    gathered = lax.all_gather(bc_in, "head", axis=0, tiled=True)
    tail_rows = jnp.concatenate(
        [x_in[tok_rows - rim_rows :].T, gathered[:, tok_rows - rim_rows :]], 0
    )
    before = from_behind(tail_rows, "ctx", 1)
    x_prev = before[:hid_cols].T
    bc_pad = jnp.concatenate([before[hid_cols:], gathered], 1)
    bcconv = jax.nn.silu(conv_cols(bc_pad, conv_bc, tok_rows)).astype(jnp.bfloat16)
    x_pad = jnp.concatenate([x_prev, x_in], 0)
    xconv = jax.nn.silu(conv_rows(x_pad, conv_x, tok_rows)).astype(jnp.bfloat16)
    delta_t = jax.nn.softplus(dt_in + dt_bias[:, None])
    log_step = -delta_t * decay_rate[:, None]
    blocks = tok_rows // SPAN
    x_blocks = xconv.reshape(blocks, SPAN, head_count, P_SIZE)
    b_blocks = bcconv[:N].reshape(N, blocks, SPAN)
    c_blocks = bcconv[N:].reshape(N, blocks, SPAN)
    dt_blocks = delta_t.reshape(head_count, blocks, SPAN)
    step_blocks = log_step.reshape(head_count, blocks, SPAN)
    cum_log, local_y, states = jax.vmap(block_local, in_axes=(0, 1, 1, 1, 1))(
        x_blocks, b_blocks, c_blocks, dt_blocks, step_blocks
    )
    keep = jnp.broadcast_to(jnp.exp(cum_log[0, :, -1:]), (head_count, N))
    quarters = states[0].reshape(head_count, 2, 2, P_SIZE // 4, N).transpose(1, 2, 0, 3, 4)
    entering = entering_states(quarters.astype(jnp.bfloat16), keep)
    carried = jnp.einsum(
        "nt,xyhpn->thxyp", c_blocks[:, 0], entering, preferred_element_type=jnp.float32
    ).reshape(tok_rows, head_count, P_SIZE)
    carried = carried * jnp.exp(cum_log[0]).T[:, :, None]
    y_total = local_y[0] + carried + d_skip[None, :, None] * x_blocks[0].astype(jnp.float32)
    gated_y = y_total.reshape(tok_rows, hid_cols) * jax.nn.silu(z_in.astype(jnp.float32))
    squares = lax.psum(jnp.sum(gated_y * gated_y, axis=1), "head")
    inverse = lax.rsqrt(squares / (HEADS * P_SIZE) + EPSILON)
    hidden = (gated_y * norm_gain[None, :]).astype(jnp.bfloat16)
    ranks = lax.axis_size("head")
    rank = lax.axis_index("head")
    share = w_out.shape[1] // ranks

    def project(owner):
        rows = lax.dynamic_slice_in_dim(w_out, owner * share, share, 1)
        return lax.dot_general(
            rows, hidden, (((0,), (1,)), ((), ())), preferred_element_type=jnp.float32
        ).astype(jnp.bfloat16)

    total = None
    arrived = []
    for shift in range(1, ranks):
        piece = project(lax.rem(rank + shift, ranks))
        arrived.append(
            lax.ppermute(piece, "head", [(i, (i + shift) % ranks) for i in range(ranks)])
        )
    total = project(rank).astype(jnp.float32)
    for piece in arrived:
        total = total + piece.astype(jnp.float32)
    return (total * inverse[None, :]).astype(jnp.bfloat16)


def solution(mesh):
    in_specs = (
        P("ctx", "head"),
        P("ctx", "head"),
        P("head", "ctx"),
        P("head", "ctx"),
        P("head"),
        P("head"),
        P("head"),
        P(None, "head"),
        P(),
        P("head"),
        P("head", None),
    )
    out_specs = P("head", "ctx")
    return jax.shard_map(
        on_device, mesh=mesh, in_specs=in_specs, out_specs=out_specs, check_vma=False
    )
```

```python
import functools

import jax
import jax.numpy as jnp
from jax import lax
from jax.experimental import pallas as pl
from jax.experimental.pallas import tpu as pltpu
from jax.sharding import PartitionSpec as P

HEADS = 80
N = 128
P_SIZE = 64
KCONV = 4
SPAN = 256


EPSILON = 1e-05
MESH = pl.DeviceIdType.MESH


def from_behind(value, axis, steps):
    count = lax.axis_size(axis)
    first, last = (max(0, -steps), min(count, count - steps))
    return lax.ppermute(value, axis, [(source, source + steps) for source in range(first, last)])


def scan_kernel(
    groups, parts, s_ref, k_ref, e_ref,
    ra, rka, tb, ktb, rb, rkb, sc, rc, sd, rd, oe, se, send, recv, ksend, krecv,
):
    idx = lax.axis_index("ctx")
    hd = lax.axis_index("head")
    c = lax.rem(idx, 2)
    x = lax.rem(lax.div(idx, 2), 2)
    g = lax.div(idx, 4)
    core_peer = idx + 1 - 2 * c
    x_peer = idx + 2 - 4 * x
    has_prev = g > 0
    has_next = g < groups - 1
    heads = k_ref.shape[0]
    size = heads // parts

    barrier = pltpu.get_barrier_semaphore()
    pl.semaphore_signal(barrier, inc=1, device_id=(core_peer, hd), device_id_type=MESH)
    pl.semaphore_signal(barrier, inc=1, device_id=(x_peer, hd), device_id_type=MESH)

    @pl.when(has_prev)
    def _():
        pl.semaphore_signal(barrier, inc=1, device_id=(idx - 4, hd), device_id_type=MESH)

    @pl.when(has_next)
    def _():
        pl.semaphore_signal(barrier, inc=1, device_id=(idx + 4, hd), device_id_type=MESH)

    pl.semaphore_wait(barrier, 2 + has_prev.astype(jnp.int32) + has_next.astype(jnp.int32))

    def copy(src, dst, phase, j, dev):
        return pltpu.make_async_remote_copy(
            src_ref=src, dst_ref=dst, send_sem=send.at[phase, j], recv_sem=recv.at[phase, j],
            device_id=(dev, hd), device_id_type=MESH,
        )

    def keep_copy(src, dst, j, dev):
        return pltpu.make_async_remote_copy(
            src_ref=src, dst_ref=dst, send_sem=ksend.at[j], recv_sem=krecv.at[j],
            device_id=(dev, hd), device_id_type=MESH,
        )

    part = [pl.ds(j * size, size) for j in range(parts)]
    f32, bf16 = jnp.float32, jnp.bfloat16
    ka = keep_copy(k_ref, rka, 0, core_peer)
    ka.start()
    step_a = [copy(s_ref.at[1 - c, :, d], ra.at[:, d], 0, j, core_peer) for j, d in enumerate(part)]
    for cp in step_a:
        cp.start()

    @pl.when(jnp.logical_not(has_prev))
    def _():
        rc[...] = jnp.zeros_like(rc)

    ka.wait_recv()
    ktb[...] = k_ref[...] * rka[...]
    kb = keep_copy(ktb, rkb, 1, x_peer)
    kb.start()
    is_core0 = c == 0
    is_x0 = x == 0

    step_b = [copy(tb.at[1 - x, d], rb.at[d], 1, j, x_peer) for j, d in enumerate(part)]
    for j, d in enumerate(part):
        step_a[j].wait_recv()
        own = s_ref[c, :, d].astype(f32)
        peer = ra[:, d].astype(f32)
        first = jnp.where(is_core0, own, peer)
        second = jnp.where(is_core0, peer, own)
        keep = jnp.where(is_core0, rka[d], k_ref[d])
        tb[:, d] = (keep[None, :, None, :] * first + second).astype(bf16)
        step_b[j].start()

    kb.wait_recv()
    step_c = [copy(sc.at[d], rc.at[d], 2, j, idx + 4) for j, d in enumerate(part)]
    step_d = [copy(sd.at[d], rd.at[d], 3, j, x_peer) for j, d in enumerate(part)]
    for j, d in enumerate(part):
        step_b[j].wait_recv()
        own = tb[x, d].astype(f32)
        peer = rb[d].astype(f32)
        first = jnp.where(is_x0, own, peer)
        second = jnp.where(is_x0, peer, own)
        keep0 = jnp.where(is_x0, ktb[d], rkb[d])[:, None, :]
        keep1 = jnp.where(is_x0, rkb[d], ktb[d])[:, None, :]

        @pl.when(has_prev)
        def _():
            step_c[j].wait_recv()

        entry = rc[d].astype(f32)
        after = keep0 * entry + first

        @pl.when(has_next)
        def _():
            sc[d] = (keep1 * after + second).astype(bf16)
            step_c[j].start()

        sd[d] = jnp.where(is_x0, after, entry).astype(bf16)
        step_d[j].start()
        oe[d] = jnp.where(is_x0, entry, after).astype(bf16)

    step_e = [copy(se.at[:, d], e_ref.at[c, :, d], 4, j, core_peer) for j, d in enumerate(part)]
    for j, d in enumerate(part):
        step_d[j].wait_recv()
        keep = jnp.where(is_core0, k_ref[d], rka[d])[:, None, :]
        for quarter, source in ((x, oe), (1 - x, rd)):
            entry = source[d].astype(f32)
            mine = jnp.where(is_core0, s_ref[c, quarter, d].astype(f32), ra[quarter, d].astype(f32))
            after = keep * entry + mine
            e_ref[c, quarter, d] = jnp.where(is_core0, entry, after).astype(bf16)
            se[quarter, d] = jnp.where(is_core0, after, entry).astype(bf16)
        step_e[j].start()

    for cp in step_e:
        cp.wait_recv()
    ka.wait_send()
    kb.wait_send()
    for j in range(parts):
        step_a[j].wait_send()
        step_b[j].wait_send()
        step_d[j].wait_send()
        step_e[j].wait_send()

    @pl.when(has_next)
    def _():
        for cp in step_c:
            cp.wait_send()


def entering_states(states, keep):
    heads = keep.shape[0]
    groups = lax.axis_size("ctx") // 4
    parts = 5
    quarter = (heads,) + states.shape[3:]
    vmem = pl.BlockSpec(memory_space=pltpu.VMEM)
    bf = jnp.bfloat16
    return pl.pallas_call(
        functools.partial(scan_kernel, groups, parts),
        out_shape=jax.ShapeDtypeStruct(states.shape, bf),
        in_specs=[vmem, vmem],
        out_specs=vmem,
        scratch_shapes=[
            pltpu.VMEM((2,) + quarter, bf),
            pltpu.VMEM(keep.shape, jnp.float32),
            pltpu.VMEM((2,) + quarter, bf),
            pltpu.VMEM(keep.shape, jnp.float32),
            pltpu.VMEM(quarter, bf),
            pltpu.VMEM(keep.shape, jnp.float32),
            pltpu.VMEM(quarter, bf),
            pltpu.VMEM(quarter, bf),
            pltpu.VMEM(quarter, bf),
            pltpu.VMEM(quarter, bf),
            pltpu.VMEM(quarter, bf),
            pltpu.VMEM((2,) + quarter, bf),
            pltpu.SemaphoreType.DMA((5, parts)),
            pltpu.SemaphoreType.DMA((5, parts)),
            pltpu.SemaphoreType.DMA((2,)),
            pltpu.SemaphoreType.DMA((2,)),
        ],
        compiler_params=pltpu.CompilerParams(
            collective_id=0, has_side_effects=True, vmem_limit_bytes=32 * 1024 * 1024
        ),
    )(states, keep)


STEPS = 5


def silu(v):
    return v / (1.0 + jnp.exp(-v))


def local_kernel(
    x_ref, xt_ref, bc_ref, bct_ref, dt_ref, bias_ref, rate_ref, skip_ref, cx_ref, cbc_ref,
    y_ref, st_ref, keep_ref, ec_ref, c_ref, cum_s, delta_s, score_s, b_s,
):
    f32, bf16 = jnp.float32, jnp.bfloat16
    step = pl.program_id(0)
    heads = dt_ref.shape[0]
    block = heads // STEPS
    length = x_ref.shape[0]

    @pl.when(step == 0)
    def _():
        lead = bct_ref.shape[1]
        wide = jnp.concatenate([bct_ref[...], bc_ref[...]], 1).astype(f32)
        summed = jnp.zeros(bc_ref.shape, f32)
        for k in range(KCONV):
            first = lead - KCONV + 1 + k
            summed = summed + cbc_ref[:, k : k + 1] * wide[:, first : first + length]
        bcconv = silu(summed)
        b_s[...] = bcconv[:N].astype(bf16)
        c_ref[...] = bcconv[N:].astype(bf16)
        c_rows = bcconv[N:].T.astype(bf16)
        scores = jnp.dot(c_rows, b_s[...], preferred_element_type=f32)
        rows = lax.broadcasted_iota(jnp.int32, (length, length), 0)
        cols = lax.broadcasted_iota(jnp.int32, (length, length), 1)
        score_s[...] = jnp.where(rows >= cols, scores, 0.0)
        raw = dt_ref[...] + bias_ref[...]
        delta = jnp.maximum(raw, 0.0) + jnp.log1p(jnp.exp(-jnp.abs(raw)))
        upper = jnp.where(rows <= cols, 1.0, 0.0)
        cum = jnp.dot(
            -delta * rate_ref[...], upper,
            precision=lax.Precision.HIGHEST, preferred_element_type=f32,
        )
        keep_ref[...] = jnp.broadcast_to(jnp.exp(cum[:, length - 1 : length]), keep_ref.shape)
        grown = jnp.exp(cum)
        for i in range(STEPS):
            part = slice(i * block, (i + 1) * block)
            cum_s[i, 0:block] = cum[part]
            delta_s[i, 0:block] = delta[part]
            ec_ref[i, 0:block] = grown[part]

    lead = xt_ref.shape[0]
    cum8 = cum_s[step]
    delta8 = delta_s[step]
    cum_cols = cum8.T
    tail8 = jnp.exp(cum8[:, length - 1 : length] - cum8) * delta8
    scores = score_s[...]
    b_rows = b_s[...]
    for j in range(block // 2):
        lanes = slice(j * 128, (j + 1) * 128)
        wide = jnp.concatenate([xt_ref[:, lanes].astype(f32), x_ref[:, lanes].astype(f32)], 0)
        summed = jnp.zeros((length, 128), f32)
        for k in range(KCONV):
            first = lead - KCONV + 1 + k
            summed = summed + cx_ref[k : k + 1, lanes] * wide[first : first + length]
        pair = silu(summed).astype(bf16)
        pair32 = pair.astype(f32)
        weights = []
        for h in (2 * j, 2 * j + 1):
            gap = jnp.minimum(cum_cols[:, h : h + 1] - cum8[h : h + 1], 0.0)
            weights.append((scores * jnp.exp(gap) * delta8[h : h + 1]).astype(bf16))
        left = lax.broadcasted_iota(jnp.int32, (length, 128), 1) < P_SIZE
        both = jnp.concatenate(
            [jnp.where(left, pair32, 0.0), jnp.where(left, 0.0, pair32)], 0
        ).astype(bf16)
        local = jnp.dot(jnp.concatenate(weights, 1), both, preferred_element_type=f32)
        y_ref[:, lanes] = local + skip_ref[:, lanes] * pair32
        flipped = pair32.T
        for half in range(2):
            h = 2 * j + half
            scaled = (flipped[half * P_SIZE : (half + 1) * P_SIZE] * tail8[h : h + 1]).astype(bf16)
            state = lax.dot_general(
                scaled, b_rows, (((1,), (1,)), ((), ())), preferred_element_type=f32
            ).astype(bf16)
            for quarter in range(4):
                st_ref[quarter // 2, quarter % 2, h] = state[quarter * 16 : (quarter + 1) * 16]


def local_terms(x_in, x_tail, bc, bc_tail, dt_in, dt_bias, decay_rate, d_skip, conv_x, conv_bc):
    length, width = x_in.shape
    heads = width // P_SIZE
    block = heads // STEPS
    cols = block * P_SIZE
    f32, bf16 = jnp.float32, jnp.bfloat16

    def whole(a):
        return pl.BlockSpec(a.shape, lambda i: (0,) * len(a.shape))

    def columns(rows):
        return pl.BlockSpec((rows, cols), lambda i: (0, i))

    args = (
        x_in, x_tail, bc, bc_tail, dt_in, dt_bias[:, None], decay_rate[:, None],
        jnp.repeat(d_skip, P_SIZE)[None, :], conv_x, conv_bc,
    )
    in_specs = [columns(length), columns(x_tail.shape[0])] + [whole(a) for a in args[2:7]]
    in_specs += [columns(1), columns(KCONV), whole(conv_bc)]
    outs = [
        jax.ShapeDtypeStruct((length, width), f32),
        jax.ShapeDtypeStruct((2, 2, heads, P_SIZE // 4, N), bf16),
        jax.ShapeDtypeStruct((heads, N), f32),
        jax.ShapeDtypeStruct((STEPS, 8, length), f32),
        jax.ShapeDtypeStruct((N, length), bf16),
    ]
    out_specs = [
        columns(length),
        pl.BlockSpec((2, 2, block, P_SIZE // 4, N), lambda i: (0, 0, i, 0, 0)),
    ] + [whole(a) for a in outs[2:]]
    return pl.pallas_call(
        local_kernel,
        out_shape=outs,
        grid=(STEPS,),
        in_specs=in_specs,
        out_specs=out_specs,
        scratch_shapes=[
            pltpu.VMEM((STEPS, 8, length), f32),
            pltpu.VMEM((STEPS, 8, length), f32),
            pltpu.VMEM((length, length), f32),
            pltpu.VMEM((N, length), bf16),
        ],
        compiler_params=pltpu.CompilerParams(vmem_limit_bytes=32 * 1024 * 1024),
    )(*args)


def gate_kernel(y_ref, z_ref, e_ref, ec_ref, c_ref, gain_ref, hid_ref, sq_ref):
    f32, bf16 = jnp.float32, jnp.bfloat16
    length, cols = y_ref.shape
    grown = ec_ref[0]
    c_cols = c_ref[...]
    squares = jnp.zeros((length, 128), f32)
    for j in range(cols // 128):
        lanes = slice(j * 128, (j + 1) * 128)
        entry = jnp.concatenate(
            [e_ref[q // 2, q % 2, h] for h in (2 * j, 2 * j + 1) for q in range(4)], 0
        )
        carried = jnp.dot(entry, c_cols, preferred_element_type=f32)
        carried = jnp.concatenate(
            [
                carried[:P_SIZE] * grown[2 * j : 2 * j + 1],
                carried[P_SIZE:] * grown[2 * j + 1 : 2 * j + 2],
            ],
            0,
        ).T
        gated = (y_ref[:, lanes] + carried) * silu(z_ref[:, lanes].astype(f32))
        squares = squares + gated * gated
        hid_ref[:, lanes] = (gated * gain_ref[:, lanes]).astype(bf16)
    summed = lax.dot_general(
        jnp.ones((8, 128), f32), squares, (((1,), (1,)), ((), ())),
        precision=lax.Precision.HIGHEST, preferred_element_type=f32,
    )

    @pl.when(pl.program_id(0) == 0)
    def _():
        sq_ref[...] = summed

    @pl.when(pl.program_id(0) > 0)
    def _():
        sq_ref[...] += summed


def gated_hidden(y, z_in, entering, grown, c_cols, norm_gain):
    length, width = y.shape
    block = width // P_SIZE // STEPS
    cols = block * P_SIZE

    def columns(rows):
        return pl.BlockSpec((rows, cols), lambda i: (0, i))

    return pl.pallas_call(
        gate_kernel,
        out_shape=[
            jax.ShapeDtypeStruct((length, width), jnp.bfloat16),
            jax.ShapeDtypeStruct((8, length), jnp.float32),
        ],
        grid=(STEPS,),
        in_specs=[
            columns(length),
            columns(length),
            pl.BlockSpec((2, 2, block, P_SIZE // 4, N), lambda i: (0, 0, i, 0, 0)),
            pl.BlockSpec((1, 8, length), lambda i: (i, 0, 0)),
            pl.BlockSpec(c_cols.shape, lambda i: (0, 0)),
            columns(1),
        ],
        out_specs=[columns(length), pl.BlockSpec((8, length), lambda i: (0, 0))],
        compiler_params=pltpu.CompilerParams(vmem_limit_bytes=32 * 1024 * 1024),
    )(y, z_in, entering, grown, c_cols, norm_gain[None, :])


CHUNK = 256


def project_kernel(
    chunks, hid_ref, sq_ref, w_ref, own_ref, got_ref, inv_ref,
    w_s, send_s, sq_s, load, send, recv, sq_sem,
):
    f32, bf16 = jnp.float32, jnp.bfloat16
    ctx = lax.axis_index("ctx")
    rank = lax.axis_index("head")
    peer = 1 - rank
    share = chunks * CHUNK
    loads = []
    for i in range(2 * chunks):
        base = (peer if i < chunks else rank) * share + (i % chunks) * CHUNK
        base = pl.multiple_of(base, CHUNK)
        cp = pltpu.make_async_copy(w_ref.at[:, pl.ds(base, CHUNK)], w_s.at[i], load.at[i])
        cp.start()
        loads.append(cp)
    barrier = pltpu.get_barrier_semaphore()
    pl.semaphore_signal(barrier, inc=1, device_id=(ctx, peer), device_id_type=MESH)
    pl.semaphore_wait(barrier, 1)
    squares = pltpu.make_async_remote_copy(
        src_ref=sq_ref, dst_ref=sq_s, send_sem=sq_sem.at[0], recv_sem=sq_sem.at[1],
        device_id=(ctx, peer), device_id_type=MESH,
    )
    squares.start()
    copies = []
    for i in range(2 * chunks):
        loads[i].wait()
        part = jnp.dot(hid_ref[...], w_s[i], preferred_element_type=f32)
        flipped = part.T.astype(bf16)
        j = i % chunks
        rows = pl.ds(j * CHUNK, CHUNK)
        if i < chunks:
            send_s[j] = flipped
            cp = pltpu.make_async_remote_copy(
                src_ref=send_s.at[j], dst_ref=got_ref.at[rows],
                send_sem=send.at[j], recv_sem=recv.at[j],
                device_id=(ctx, peer), device_id_type=MESH,
            )
            cp.start()
            copies.append(cp)
        else:
            own_ref[rows] = flipped
    squares.wait()
    inv_ref[...] = lax.rsqrt((sq_ref[...] + sq_s[...]) / (HEADS * P_SIZE) + EPSILON)
    for cp in copies:
        cp.wait()


def project_pair(hidden, squares, w_out):
    length = hidden.shape[0]
    depth, width = w_out.shape
    chunks = width // 2 // CHUNK
    half = jax.ShapeDtypeStruct((width // 2, length), jnp.bfloat16)
    vmem = pl.BlockSpec(memory_space=pltpu.VMEM)
    own, got, inverse = pl.pallas_call(
        functools.partial(project_kernel, chunks),
        out_shape=[half, half, jax.ShapeDtypeStruct(squares.shape, jnp.float32)],
        in_specs=[vmem, vmem, pl.BlockSpec(memory_space=pl.ANY)],
        out_specs=[vmem] * 3,
        scratch_shapes=[
            pltpu.VMEM((2 * chunks, depth, CHUNK), jnp.bfloat16),
            pltpu.VMEM((chunks, CHUNK, length), jnp.bfloat16),
            pltpu.VMEM(squares.shape, jnp.float32),
            pltpu.SemaphoreType.DMA((2 * chunks,)),
            pltpu.SemaphoreType.DMA((chunks,)),
            pltpu.SemaphoreType.DMA((chunks,)),
            pltpu.SemaphoreType.DMA((2,)),
        ],
        compiler_params=pltpu.CompilerParams(
            collective_id=1, has_side_effects=True, vmem_limit_bytes=40 * 1024 * 1024
        ),
    )(hidden, squares, w_out)
    total = own.astype(jnp.float32) + got.astype(jnp.float32)
    return (total * inverse[:1]).astype(jnp.bfloat16)


def project_any(hidden, squares, w_out):
    inverse = lax.rsqrt(lax.psum(squares[0], "head") / (HEADS * P_SIZE) + EPSILON)
    ranks = lax.axis_size("head")
    rank = lax.axis_index("head")
    share = w_out.shape[1] // ranks

    def project(owner):
        rows = lax.dynamic_slice_in_dim(w_out, owner * share, share, 1)
        return lax.dot_general(
            rows, hidden, (((0,), (1,)), ((), ())), preferred_element_type=jnp.float32
        ).astype(jnp.bfloat16)

    arrived = []
    for shift in range(1, ranks):
        piece = project(lax.rem(rank + shift, ranks))
        arrived.append(
            lax.ppermute(piece, "head", [(i, (i + shift) % ranks) for i in range(ranks)])
        )
    total = project(rank).astype(jnp.float32)
    for piece in arrived:
        total = total + piece.astype(jnp.float32)
    return (total * inverse[None, :]).astype(jnp.bfloat16)


def on_device(
    x_in, z_in, bc_in, dt_in, dt_bias, decay_rate, d_skip, conv_x, conv_bc, norm_gain, w_out
):
    tok_rows = x_in.shape[0]
    hid_cols = x_in.shape[1]
    bc = lax.all_gather(bc_in, "head", axis=0, tiled=True)
    tails = jnp.concatenate([x_in[tok_rows - 16 :].reshape(-1, 128), bc[:, tok_rows - 128 :]], 0)
    before = from_behind(tails, "ctx", 1)
    x_tail = before[: hid_cols // 8].reshape(16, hid_cols)
    bc_tail = before[hid_cols // 8 :]
    y, states, keep, grown, c_cols = local_terms(
        x_in, x_tail, bc, bc_tail, dt_in, dt_bias, decay_rate, d_skip, conv_x, conv_bc
    )
    entering = entering_states(states, keep)
    hidden, squares = gated_hidden(y, z_in, entering, grown, c_cols, norm_gain)
    if lax.axis_size("head") == 2 and w_out.shape[1] % (2 * CHUNK) == 0:
        return project_pair(hidden, squares, w_out)
    return project_any(hidden, squares, w_out)


def solution(mesh):
    in_specs = (
        P("ctx", "head"),
        P("ctx", "head"),
        P("head", "ctx"),
        P("head", "ctx"),
        P("head"),
        P("head"),
        P("head"),
        P(None, "head"),
        P(),
        P("head"),
        P("head", None),
    )
    out_specs = P("head", "ctx")
    return jax.shard_map(
        on_device, mesh=mesh, in_specs=in_specs, out_specs=out_specs, check_vma=False
    )
```

```python
import functools

import jax
import jax.numpy as jnp
from jax import lax
from jax.experimental import pallas as pl
from jax.experimental.pallas import tpu as pltpu
from jax.sharding import PartitionSpec as P

HEADS = 80
N = 128
P_SIZE = 64
KCONV = 4
SPAN = 256


EPSILON = 1e-05
MESH = pl.DeviceIdType.MESH


def from_behind(value, axis, steps):
    count = lax.axis_size(axis)
    first, last = (max(0, -steps), min(count, count - steps))
    return lax.ppermute(value, axis, [(source, source + steps) for source in range(first, last)])


STEPS = 5
CHUNK = 256


def silu(v):
    return v / (1.0 + jnp.exp(-v))


def mixer_kernel(
    groups, chunks, s_ref, k_ref, xc_ref, score_ref, cum_ref, delta_ref, c_ref, skip_ref, gain_ref,
    z_ref, w_ref, *rest,
):
    if chunks:
        own_ref, got_ref, inv_ref, *rest = rest
        w_s, send_s, sq_s, sq_own, hid_s, load, psend, precv, sq_sem, *rest = rest
    else:
        hid_s, sq_own, *rest = rest
    (
        z_s, z_sem, y_s, e_s, ra, rka, tb, ktb, rb, rkb, sc, rc, sd, rd, oe, se,
        send, recv, ksend, krecv,
    ) = rest
    f32, bf16 = jnp.float32, jnp.bfloat16
    idx = lax.axis_index("ctx")
    hd = lax.axis_index("head")
    c = lax.rem(idx, 2)
    x = lax.rem(lax.div(idx, 2), 2)
    g = lax.div(idx, 4)
    core_peer = idx + 1 - 2 * c
    x_peer = idx + 2 - 4 * x
    has_prev = g > 0
    has_next = g < groups - 1
    heads = k_ref.shape[0]
    size = heads // STEPS
    cols = size * P_SIZE
    length = xc_ref.shape[0]

    barrier = pltpu.get_barrier_semaphore()
    pl.semaphore_signal(barrier, inc=1, device_id=(core_peer, hd), device_id_type=MESH)
    pl.semaphore_signal(barrier, inc=1, device_id=(x_peer, hd), device_id_type=MESH)
    if chunks:
        pl.semaphore_signal(barrier, inc=1, device_id=(idx, 1 - hd), device_id_type=MESH)

    @pl.when(has_prev)
    def _():
        pl.semaphore_signal(barrier, inc=1, device_id=(idx - 4, hd), device_id_type=MESH)

    @pl.when(has_next)
    def _():
        pl.semaphore_signal(barrier, inc=1, device_id=(idx + 4, hd), device_id_type=MESH)

    z_load = pltpu.make_async_copy(z_ref, z_s, z_sem.at[0])
    z_load.start()
    loads = []
    for i in range(2 * chunks):
        base = (1 - hd if i < chunks else hd) * (chunks * CHUNK) + (i % chunks) * CHUNK
        base = pl.multiple_of(base, CHUNK)
        cp = pltpu.make_async_copy(w_ref.at[:, pl.ds(base, CHUNK)], w_s.at[i], load.at[i])
        cp.start()
        loads.append(cp)

    greeted = 3 if chunks else 2
    pl.semaphore_wait(barrier, greeted + has_prev.astype(jnp.int32) + has_next.astype(jnp.int32))

    def copy(src, dst, phase, j, dev):
        return pltpu.make_async_remote_copy(
            src_ref=src, dst_ref=dst, send_sem=send.at[phase, j], recv_sem=recv.at[phase, j],
            device_id=(dev, hd), device_id_type=MESH,
        )

    def keep_copy(src, dst, j, dev):
        return pltpu.make_async_remote_copy(
            src_ref=src, dst_ref=dst, send_sem=ksend.at[j], recv_sem=krecv.at[j],
            device_id=(dev, hd), device_id_type=MESH,
        )

    part = [pl.ds(j * size, size) for j in range(STEPS)]
    ka = keep_copy(k_ref, rka, 0, core_peer)
    ka.start()
    step_a = [copy(s_ref.at[1 - c, :, d], ra.at[:, d], 0, j, core_peer) for j, d in enumerate(part)]
    for cp in step_a:
        cp.start()

    @pl.when(jnp.logical_not(has_prev))
    def _():
        rc[...] = jnp.zeros_like(rc)

    def local_chunks(low, high):
        @pl.loop(low, high)
        def _(i):
            cum8 = cum_ref[i]
            delta8 = delta_ref[i]
            cum_cols = cum8.T
            scores = score_ref[...]
            left = lax.broadcasted_iota(jnp.int32, (length, 128), 1) < P_SIZE
            for j in range(size // 2):
                lanes = pl.ds(pl.multiple_of(i * cols + j * 128, 128), 128)
                pair = xc_ref[:, lanes].astype(f32)
                weights = []
                for h in (2 * j, 2 * j + 1):
                    gap = jnp.minimum(cum_cols[:, h : h + 1] - cum8[h : h + 1], 0.0)
                    weights.append((scores * jnp.exp(gap) * delta8[h : h + 1]).astype(bf16))
                both = jnp.concatenate(
                    [jnp.where(left, pair, 0.0), jnp.where(left, 0.0, pair)], 0
                ).astype(bf16)
                local = jnp.dot(jnp.concatenate(weights, 1), both, preferred_element_type=f32)
                y_s[:, lanes] = local + skip_ref[:, lanes] * pair

    early = jnp.minimum(2 + g, STEPS)
    local_chunks(0, 1)

    ka.wait_recv()
    ktb[...] = k_ref[...] * rka[...]
    kb = keep_copy(ktb, rkb, 1, x_peer)
    kb.start()
    is_core0 = c == 0
    is_x0 = x == 0

    step_b = [copy(tb.at[1 - x, d], rb.at[d], 1, j, x_peer) for j, d in enumerate(part)]
    for j, d in enumerate(part):
        step_a[j].wait_recv()
        own = s_ref[c, :, d].astype(f32)
        peer = ra[:, d].astype(f32)
        first = jnp.where(is_core0, own, peer)
        second = jnp.where(is_core0, peer, own)
        keep = jnp.where(is_core0, rka[d], k_ref[d])
        tb[:, d] = (keep[None, :, None, :] * first + second).astype(bf16)
        step_b[j].start()

    local_chunks(1, early)

    kb.wait_recv()
    step_c = [copy(sc.at[d], rc.at[d], 2, j, idx + 4) for j, d in enumerate(part)]
    step_d = [copy(sd.at[d], rd.at[d], 3, j, x_peer) for j, d in enumerate(part)]
    for j, d in enumerate(part):
        step_b[j].wait_recv()
        own = tb[x, d].astype(f32)
        peer = rb[d].astype(f32)
        first = jnp.where(is_x0, own, peer)
        second = jnp.where(is_x0, peer, own)
        keep0 = jnp.where(is_x0, ktb[d], rkb[d])[:, None, :]
        keep1 = jnp.where(is_x0, rkb[d], ktb[d])[:, None, :]

        @pl.when(has_prev)
        def _():
            step_c[j].wait_recv()

        entry = rc[d].astype(f32)
        after = keep0 * entry + first

        @pl.when(has_next)
        def _():
            sc[d] = (keep1 * after + second).astype(bf16)
            step_c[j].start()

        sd[d] = jnp.where(is_x0, after, entry).astype(bf16)
        step_d[j].start()
        oe[d] = jnp.where(is_x0, entry, after).astype(bf16)

    local_chunks(early, STEPS)
    z_load.wait()

    step_e = [copy(se.at[:, d], e_s.at[c, :, d], 4, j, core_peer) for j, d in enumerate(part)]
    squares = jnp.zeros((length, 128), f32)
    c_cols = c_ref[...]
    for j in range(STEPS + 1):
        if j < STEPS:
            d = part[j]
            step_d[j].wait_recv()
            keep = jnp.where(is_core0, k_ref[d], rka[d])[:, None, :]
            for quarter, source in ((x, oe), (1 - x, rd)):
                entry = source[d].astype(f32)
                mine = jnp.where(
                    is_core0, s_ref[c, quarter, d].astype(f32), ra[quarter, d].astype(f32)
                )
                after = keep * entry + mine
                e_s[c, quarter, d] = jnp.where(is_core0, entry, after).astype(bf16)
                se[quarter, d] = jnp.where(is_core0, after, entry).astype(bf16)
            step_e[j].start()
        if j > 0:
            i = j - 1
            step_e[i].wait_recv()
            grown = jnp.exp(cum_ref[i])
            for n in range(size // 2):
                lanes = slice(i * cols + n * 128, i * cols + (n + 1) * 128)
                entry = jnp.concatenate(
                    [
                        e_s[q // 2, q % 2, i * size + h]
                        for h in (2 * n, 2 * n + 1)
                        for q in range(4)
                    ],
                    0,
                )
                carried = jnp.dot(entry, c_cols, preferred_element_type=f32)
                carried = jnp.concatenate(
                    [
                        carried[:P_SIZE] * grown[2 * n : 2 * n + 1],
                        carried[P_SIZE:] * grown[2 * n + 1 : 2 * n + 2],
                    ],
                    0,
                ).T
                gated = (y_s[:, lanes] + carried) * silu(z_s[:, lanes].astype(f32))
                squares = squares + gated * gated
                hid_s[:, lanes] = (gated * gain_ref[:, lanes]).astype(bf16)

    sq_own[...] = lax.dot_general(
        jnp.ones((8, 128), f32), squares, (((1,), (1,)), ((), ())),
        precision=lax.Precision.HIGHEST, preferred_element_type=f32,
    )
    if chunks:
        sq_copy = pltpu.make_async_remote_copy(
            src_ref=sq_own, dst_ref=sq_s, send_sem=sq_sem.at[0], recv_sem=sq_sem.at[1],
            device_id=(idx, 1 - hd), device_id_type=MESH,
        )
        sq_copy.start()
        copies = []
        for i in range(2 * chunks):
            loads[i].wait()
            flipped = jnp.dot(hid_s[...], w_s[i], preferred_element_type=f32).T.astype(bf16)
            j = i % chunks
            rows = pl.ds(j * CHUNK, CHUNK)
            if i < chunks:
                send_s[j] = flipped
                cp = pltpu.make_async_remote_copy(
                    src_ref=send_s.at[j], dst_ref=got_ref.at[rows],
                    send_sem=psend.at[j], recv_sem=precv.at[j],
                    device_id=(idx, 1 - hd), device_id_type=MESH,
                )
                cp.start()
                copies.append(cp)
            else:
                own_ref[rows] = flipped
        sq_copy.wait()
        inv_ref[...] = lax.rsqrt((sq_own[...] + sq_s[...]) / (HEADS * P_SIZE) + EPSILON)
        for cp in copies:
            cp.wait()

    ka.wait_send()
    kb.wait_send()
    for j in range(STEPS):
        step_a[j].wait_send()
        step_b[j].wait_send()
        step_d[j].wait_send()
        step_e[j].wait_send()

    @pl.when(has_next)
    def _():
        for cp in step_c:
            cp.wait_send()


def mix(states, keep, xconv, scores, cum, delta, c_cols, skip, gain, z_in, w_out):
    heads = keep.shape[0]
    length, hid = xconv.shape
    depth, width = w_out.shape
    groups = lax.axis_size("ctx") // 4
    paired = lax.axis_size("head") == 2 and width % (2 * CHUNK) == 0
    chunks = width // 2 // CHUNK if paired else 0
    quarter = (heads,) + states.shape[3:]
    vmem = pl.BlockSpec(memory_space=pltpu.VMEM)
    bf, f32 = jnp.bfloat16, jnp.float32
    dma = pltpu.SemaphoreType.DMA
    rows8 = (8, length)
    if paired:
        half = jax.ShapeDtypeStruct((width // 2, length), bf)
        outs = [half, half, jax.ShapeDtypeStruct(rows8, f32)]
        scratch = [
            pltpu.VMEM((2 * chunks, depth, CHUNK), bf),
            pltpu.VMEM((chunks, CHUNK, length), bf),
            pltpu.VMEM(rows8, f32),
            pltpu.VMEM(rows8, f32),
            pltpu.VMEM((length, hid), bf),
            dma((2 * chunks,)),
            dma((chunks,)),
            dma((chunks,)),
            dma((2,)),
        ]
    else:
        outs = [jax.ShapeDtypeStruct((length, hid), bf), jax.ShapeDtypeStruct(rows8, f32)]
        scratch = []
    scratch += [
        pltpu.VMEM((length, hid), bf),
        dma((1,)),
        pltpu.VMEM((length, hid), f32),
        pltpu.VMEM(states.shape, bf),
        pltpu.VMEM((2,) + quarter, bf),
        pltpu.VMEM(keep.shape, f32),
        pltpu.VMEM((2,) + quarter, bf),
        pltpu.VMEM(keep.shape, f32),
        pltpu.VMEM(quarter, bf),
        pltpu.VMEM(keep.shape, f32),
    ]
    scratch += [pltpu.VMEM(quarter, bf)] * 5
    scratch += [
        pltpu.VMEM((2,) + quarter, bf),
        dma((5, STEPS)),
        dma((5, STEPS)),
        dma((2,)),
        dma((2,)),
    ]
    result = pl.pallas_call(
        functools.partial(mixer_kernel, groups, chunks),
        out_shape=outs,
        in_specs=[vmem] * 9 + [pl.BlockSpec(memory_space=pl.ANY)] * 2,
        out_specs=[vmem] * len(outs),
        scratch_shapes=scratch,
        compiler_params=pltpu.CompilerParams(
            collective_id=0, has_side_effects=True, vmem_limit_bytes=44 * 1024 * 1024
        ),
    )(states, keep, xconv, scores, cum, delta, c_cols, skip, gain, z_in, w_out)
    if not paired:
        return project_any(result[0], result[1], w_out)
    own, got, inverse = result
    total = own.astype(f32) + got.astype(f32)
    return (total * inverse[:1]).astype(bf)


def local_kernel(
    x_ref, xt_ref, bc_ref, bct_ref, dt_ref, bias_ref, rate_ref, cx_ref, cbc_ref,
    xc_ref, st_ref, keep_ref, score_ref, cum_ref, delta_ref, c_ref, b_s,
):
    f32, bf16 = jnp.float32, jnp.bfloat16
    step = pl.program_id(0)
    heads = dt_ref.shape[0]
    block = heads // STEPS
    length = x_ref.shape[0]

    @pl.when(step == 0)
    def _():
        lead = bct_ref.shape[1]
        wide = jnp.concatenate([bct_ref[...], bc_ref[...]], 1).astype(f32)
        summed = jnp.zeros(bc_ref.shape, f32)
        for k in range(KCONV):
            first = lead - KCONV + 1 + k
            summed = summed + cbc_ref[:, k : k + 1] * wide[:, first : first + length]
        bcconv = silu(summed)
        b_s[...] = bcconv[:N].astype(bf16)
        c_ref[...] = bcconv[N:].astype(bf16)
        c_rows = bcconv[N:].T.astype(bf16)
        scores = jnp.dot(c_rows, b_s[...], preferred_element_type=f32)
        rows = lax.broadcasted_iota(jnp.int32, (length, length), 0)
        cols = lax.broadcasted_iota(jnp.int32, (length, length), 1)
        score_ref[...] = jnp.where(rows >= cols, scores, 0.0)
        raw = dt_ref[...] + bias_ref[...]
        delta = jnp.maximum(raw, 0.0) + jnp.log1p(jnp.exp(-jnp.abs(raw)))
        upper = jnp.where(rows <= cols, 1.0, 0.0)
        cum = jnp.dot(
            -delta * rate_ref[...], upper,
            precision=lax.Precision.HIGHEST, preferred_element_type=f32,
        )
        keep_ref[...] = jnp.broadcast_to(jnp.exp(cum[:, length - 1 : length]), keep_ref.shape)
        for i in range(STEPS):
            part = slice(i * block, (i + 1) * block)
            cum_ref[i, 0:block] = cum[part]
            delta_ref[i, 0:block] = delta[part]

    lead = xt_ref.shape[0]
    cum8 = cum_ref[step]
    delta8 = delta_ref[step]
    tail8 = jnp.exp(cum8[:, length - 1 : length] - cum8) * delta8
    b_rows = b_s[...]
    for j in range(block // 2):
        lanes = slice(j * 128, (j + 1) * 128)
        wide = jnp.concatenate([xt_ref[:, lanes].astype(f32), x_ref[:, lanes].astype(f32)], 0)
        summed = jnp.zeros((length, 128), f32)
        for k in range(KCONV):
            first = lead - KCONV + 1 + k
            summed = summed + cx_ref[k : k + 1, lanes] * wide[first : first + length]
        pair = silu(summed).astype(bf16)
        xc_ref[:, lanes] = pair
        pair32 = pair.astype(f32)
        flipped = pair32.T
        for half in range(2):
            h = 2 * j + half
            scaled = (flipped[half * P_SIZE : (half + 1) * P_SIZE] * tail8[h : h + 1]).astype(bf16)
            state = lax.dot_general(
                scaled, b_rows, (((1,), (1,)), ((), ())), preferred_element_type=f32
            ).astype(bf16)
            for quarter in range(4):
                st_ref[quarter // 2, quarter % 2, h] = state[quarter * 16 : (quarter + 1) * 16]


def local_terms(x_in, x_tail, bc, bc_tail, dt_in, dt_bias, decay_rate, conv_x, conv_bc):
    length, width = x_in.shape
    heads = width // P_SIZE
    block = heads // STEPS
    cols = block * P_SIZE
    f32, bf16 = jnp.float32, jnp.bfloat16

    def whole(a):
        return pl.BlockSpec(a.shape, lambda i: (0,) * len(a.shape))

    def columns(rows):
        return pl.BlockSpec((rows, cols), lambda i: (0, i))

    args = (
        x_in, x_tail, bc, bc_tail, dt_in, dt_bias[:, None], decay_rate[:, None],
        conv_x, conv_bc,
    )
    in_specs = [columns(length), columns(x_tail.shape[0])] + [whole(a) for a in args[2:7]]
    in_specs += [columns(KCONV), whole(conv_bc)]
    outs = [
        jax.ShapeDtypeStruct((length, width), bf16),
        jax.ShapeDtypeStruct((2, 2, heads, P_SIZE // 4, N), bf16),
        jax.ShapeDtypeStruct((heads, N), f32),
        jax.ShapeDtypeStruct((length, length), f32),
        jax.ShapeDtypeStruct((STEPS, 8, length), f32),
        jax.ShapeDtypeStruct((STEPS, 8, length), f32),
        jax.ShapeDtypeStruct((N, length), bf16),
    ]
    out_specs = [
        columns(length),
        pl.BlockSpec((2, 2, block, P_SIZE // 4, N), lambda i: (0, 0, i, 0, 0)),
    ] + [whole(a) for a in outs[2:]]
    return pl.pallas_call(
        local_kernel,
        out_shape=outs,
        grid=(STEPS,),
        in_specs=in_specs,
        out_specs=out_specs,
        scratch_shapes=[
            pltpu.VMEM((N, length), bf16),
        ],
        compiler_params=pltpu.CompilerParams(vmem_limit_bytes=32 * 1024 * 1024),
    )(*args)


def project_any(hidden, squares, w_out):
    inverse = lax.rsqrt(lax.psum(squares[0], "head") / (HEADS * P_SIZE) + EPSILON)
    ranks = lax.axis_size("head")
    rank = lax.axis_index("head")
    share = w_out.shape[1] // ranks

    def project(owner):
        rows = lax.dynamic_slice_in_dim(w_out, owner * share, share, 1)
        return lax.dot_general(
            rows, hidden, (((0,), (1,)), ((), ())), preferred_element_type=jnp.float32
        ).astype(jnp.bfloat16)

    arrived = []
    for shift in range(1, ranks):
        piece = project(lax.rem(rank + shift, ranks))
        arrived.append(
            lax.ppermute(piece, "head", [(i, (i + shift) % ranks) for i in range(ranks)])
        )
    total = project(rank).astype(jnp.float32)
    for piece in arrived:
        total = total + piece.astype(jnp.float32)
    return (total * inverse[None, :]).astype(jnp.bfloat16)


def on_device(
    x_in, z_in, bc_in, dt_in, dt_bias, decay_rate, d_skip, conv_x, conv_bc, norm_gain, w_out
):
    tok_rows = x_in.shape[0]
    hid_cols = x_in.shape[1]
    bc = lax.all_gather(bc_in, "head", axis=0, tiled=True)
    tails = jnp.concatenate([x_in[tok_rows - 16 :].reshape(-1, 128), bc[:, tok_rows - 128 :]], 0)
    before = from_behind(tails, "ctx", 1)
    x_tail = before[: hid_cols // 8].reshape(16, hid_cols)
    bc_tail = before[hid_cols // 8 :]
    terms = local_terms(
        x_in, x_tail, bc, bc_tail, dt_in, dt_bias, decay_rate, conv_x, conv_bc
    )
    xconv, states, keep, scores, cum, delta, c_cols = terms
    skip = jnp.repeat(d_skip, P_SIZE)[None, :]
    return mix(
        states, keep, xconv, scores, cum, delta, c_cols, skip, norm_gain[None, :], z_in, w_out
    )


def solution(mesh):
    in_specs = (
        P("ctx", "head"),
        P("ctx", "head"),
        P("head", "ctx"),
        P("head", "ctx"),
        P("head"),
        P("head"),
        P("head"),
        P(None, "head"),
        P(),
        P("head"),
        P("head", None),
    )
    out_specs = P("head", "ctx")
    return jax.shard_map(
        on_device, mesh=mesh, in_specs=in_specs, out_specs=out_specs, check_vma=False
    )
```

```python
import functools

import jax
import jax.numpy as jnp
from jax import lax
from jax.experimental import pallas as pl
from jax.experimental.pallas import tpu as pltpu
from jax.sharding import PartitionSpec as P

HEADS = 80
N = 128
P_SIZE = 64
KCONV = 4
SPAN = 256


EPSILON = 1e-05
MESH = pl.DeviceIdType.MESH


STEPS = 5
CHUNK = 256


def silu(v):
    return v / (1.0 + jnp.exp(-v))


def mixer_kernel(
    groups, chunks, s_ref, k_ref, xc_ref, score_ref, cum_ref, delta_ref, c_ref, skip_ref, gain_ref,
    z_ref, w_ref, *rest,
):
    if chunks:
        own_ref, got_ref, inv_ref, *rest = rest
        w_s, send_s, sq_s, sq_own, hid_s, load, psend, precv, sq_sem, *rest = rest
    else:
        hid_s, sq_own, *rest = rest
    (
        z_s, z_sem, y_s, e_s, ra, rka, tb, ktb, rb, rkb, sc, rc, sd, rd, oe, se,
        send, recv, ksend, krecv,
    ) = rest
    f32, bf16 = jnp.float32, jnp.bfloat16
    idx = lax.axis_index("ctx")
    hd = lax.axis_index("head")
    c = lax.rem(idx, 2)
    x = lax.rem(lax.div(idx, 2), 2)
    g = lax.div(idx, 4)
    core_peer = idx + 1 - 2 * c
    x_peer = idx + 2 - 4 * x
    has_prev = g > 0
    has_next = g < groups - 1
    heads = k_ref.shape[0]
    size = heads // STEPS
    cols = size * P_SIZE
    length = xc_ref.shape[0]

    barrier = pltpu.get_barrier_semaphore()
    pl.semaphore_signal(barrier, inc=1, device_id=(core_peer, hd), device_id_type=MESH)
    pl.semaphore_signal(barrier, inc=1, device_id=(x_peer, hd), device_id_type=MESH)
    if chunks:
        pl.semaphore_signal(barrier, inc=1, device_id=(idx, 1 - hd), device_id_type=MESH)

    @pl.when(has_prev)
    def _():
        pl.semaphore_signal(barrier, inc=1, device_id=(idx - 4, hd), device_id_type=MESH)

    @pl.when(has_next)
    def _():
        pl.semaphore_signal(barrier, inc=1, device_id=(idx + 4, hd), device_id_type=MESH)

    z_load = pltpu.make_async_copy(z_ref, z_s, z_sem.at[0])
    z_load.start()
    loads = []
    for i in range(2 * chunks):
        base = (1 - hd if i < chunks else hd) * (chunks * CHUNK) + (i % chunks) * CHUNK
        base = pl.multiple_of(base, CHUNK)
        cp = pltpu.make_async_copy(w_ref.at[:, pl.ds(base, CHUNK)], w_s.at[i], load.at[i])
        cp.start()
        loads.append(cp)

    greeted = 3 if chunks else 2
    pl.semaphore_wait(barrier, greeted + has_prev.astype(jnp.int32) + has_next.astype(jnp.int32))

    def copy(src, dst, phase, j, dev):
        return pltpu.make_async_remote_copy(
            src_ref=src, dst_ref=dst, send_sem=send.at[phase, j], recv_sem=recv.at[phase, j],
            device_id=(dev, hd), device_id_type=MESH,
        )

    def keep_copy(src, dst, j, dev):
        return pltpu.make_async_remote_copy(
            src_ref=src, dst_ref=dst, send_sem=ksend.at[j], recv_sem=krecv.at[j],
            device_id=(dev, hd), device_id_type=MESH,
        )

    part = [pl.ds(j * size, size) for j in range(STEPS)]
    ka = keep_copy(k_ref, rka, 0, core_peer)
    ka.start()
    step_a = [copy(s_ref.at[1 - c, :, d], ra.at[:, d], 0, j, core_peer) for j, d in enumerate(part)]
    for cp in step_a:
        cp.start()

    @pl.when(jnp.logical_not(has_prev))
    def _():
        rc[...] = jnp.zeros_like(rc)

    def local_chunks(low, high):
        @pl.loop(low, high)
        def _(i):
            cum8 = cum_ref[i]
            delta8 = delta_ref[i]
            cum_cols = cum8.T
            scores = score_ref[...]
            left = lax.broadcasted_iota(jnp.int32, (length, 128), 1) < P_SIZE
            for j in range(size // 2):
                lanes = pl.ds(pl.multiple_of(i * cols + j * 128, 128), 128)
                pair = xc_ref[:, lanes].astype(f32)
                weights = []
                for h in (2 * j, 2 * j + 1):
                    gap = jnp.minimum(cum_cols[:, h : h + 1] - cum8[h : h + 1], 0.0)
                    weights.append((scores * jnp.exp(gap) * delta8[h : h + 1]).astype(bf16))
                both = jnp.concatenate(
                    [jnp.where(left, pair, 0.0), jnp.where(left, 0.0, pair)], 0
                ).astype(bf16)
                local = jnp.dot(jnp.concatenate(weights, 1), both, preferred_element_type=f32)
                first = i * size + 2 * j
                y_s[:, lanes] = local + jnp.where(left, skip_ref[first], skip_ref[first + 1]) * pair

    early = jnp.minimum(2 + g, STEPS)
    local_chunks(0, 1)

    ka.wait_recv()
    ktb[...] = k_ref[...] * rka[...]
    kb = keep_copy(ktb, rkb, 1, x_peer)
    kb.start()
    is_core0 = c == 0
    is_x0 = x == 0

    step_b = [copy(tb.at[1 - x, d], rb.at[d], 1, j, x_peer) for j, d in enumerate(part)]
    for j, d in enumerate(part):
        step_a[j].wait_recv()
        own = s_ref[c, :, d].astype(f32)
        peer = ra[:, d].astype(f32)
        first = jnp.where(is_core0, own, peer)
        second = jnp.where(is_core0, peer, own)
        keep = jnp.where(is_core0, rka[d], k_ref[d])
        tb[:, d] = (keep[None, :, None, :] * first + second).astype(bf16)
        step_b[j].start()

    local_chunks(1, early)

    kb.wait_recv()
    step_c = [copy(sc.at[d], rc.at[d], 2, j, idx + 4) for j, d in enumerate(part)]
    step_d = [copy(sd.at[d], rd.at[d], 3, j, x_peer) for j, d in enumerate(part)]
    for j, d in enumerate(part):
        step_b[j].wait_recv()
        own = tb[x, d].astype(f32)
        peer = rb[d].astype(f32)
        first = jnp.where(is_x0, own, peer)
        second = jnp.where(is_x0, peer, own)
        keep0 = jnp.where(is_x0, ktb[d], rkb[d])[:, None, :]
        keep1 = jnp.where(is_x0, rkb[d], ktb[d])[:, None, :]

        @pl.when(has_prev)
        def _():
            step_c[j].wait_recv()

        entry = rc[d].astype(f32)
        after = keep0 * entry + first

        @pl.when(has_next)
        def _():
            sc[d] = (keep1 * after + second).astype(bf16)
            step_c[j].start()

        sd[d] = jnp.where(is_x0, after, entry).astype(bf16)
        step_d[j].start()
        oe[d] = jnp.where(is_x0, entry, after).astype(bf16)

    local_chunks(early, STEPS)
    z_load.wait()

    step_e = [copy(se.at[:, d], e_s.at[c, :, d], 4, j, core_peer) for j, d in enumerate(part)]
    squares = jnp.zeros((length, 128), f32)
    c_cols = c_ref[...]
    for j in range(STEPS + 1):
        if j < STEPS:
            d = part[j]
            step_d[j].wait_recv()
            keep = jnp.where(is_core0, k_ref[d], rka[d])[:, None, :]
            for quarter, source in ((x, oe), (1 - x, rd)):
                entry = source[d].astype(f32)
                mine = jnp.where(
                    is_core0, s_ref[c, quarter, d].astype(f32), ra[quarter, d].astype(f32)
                )
                after = keep * entry + mine
                e_s[c, quarter, d] = jnp.where(is_core0, entry, after).astype(bf16)
                se[quarter, d] = jnp.where(is_core0, after, entry).astype(bf16)
            step_e[j].start()
        if j > 0:
            i = j - 1
            step_e[i].wait_recv()
            grown = jnp.exp(cum_ref[i])
            for n in range(size // 2):
                lanes = slice(i * cols + n * 128, i * cols + (n + 1) * 128)
                entry = jnp.concatenate(
                    [
                        e_s[q // 2, q % 2, i * size + h]
                        for h in (2 * n, 2 * n + 1)
                        for q in range(4)
                    ],
                    0,
                )
                carried = jnp.dot(entry, c_cols, preferred_element_type=f32)
                carried = jnp.concatenate(
                    [
                        carried[:P_SIZE] * grown[2 * n : 2 * n + 1],
                        carried[P_SIZE:] * grown[2 * n + 1 : 2 * n + 2],
                    ],
                    0,
                ).T
                gated = (y_s[:, lanes] + carried) * silu(z_s[:, lanes].astype(f32))
                squares = squares + gated * gated
                hid_s[:, lanes] = (gated * gain_ref[lanes][None, :]).astype(bf16)

    sq_own[...] = lax.dot_general(
        jnp.ones((8, 128), f32), squares, (((1,), (1,)), ((), ())),
        precision=lax.Precision.HIGHEST, preferred_element_type=f32,
    )
    if chunks:
        sq_copy = pltpu.make_async_remote_copy(
            src_ref=sq_own, dst_ref=sq_s, send_sem=sq_sem.at[0], recv_sem=sq_sem.at[1],
            device_id=(idx, 1 - hd), device_id_type=MESH,
        )
        sq_copy.start()
        copies = []
        for i in range(2 * chunks):
            loads[i].wait()
            flipped = jnp.dot(hid_s[...], w_s[i], preferred_element_type=f32).T.astype(bf16)
            j = i % chunks
            rows = pl.ds(j * CHUNK, CHUNK)
            if i < chunks:
                send_s[j] = flipped
                cp = pltpu.make_async_remote_copy(
                    src_ref=send_s.at[j], dst_ref=got_ref.at[rows],
                    send_sem=psend.at[j], recv_sem=precv.at[j],
                    device_id=(idx, 1 - hd), device_id_type=MESH,
                )
                cp.start()
                copies.append(cp)
            else:
                own_ref[rows] = flipped
        sq_copy.wait()
        inv_ref[...] = lax.rsqrt((sq_own[...] + sq_s[...]) / (HEADS * P_SIZE) + EPSILON)
        for cp in copies:
            cp.wait()

    ka.wait_send()
    kb.wait_send()
    for j in range(STEPS):
        step_a[j].wait_send()
        step_b[j].wait_send()
        step_d[j].wait_send()
        step_e[j].wait_send()

    @pl.when(has_next)
    def _():
        for cp in step_c:
            cp.wait_send()


def mix(states, keep, xconv, scores, cum, delta, c_cols, skip, gain, z_in, w_out):
    heads = keep.shape[0]
    length, hid = xconv.shape
    depth, width = w_out.shape
    groups = lax.axis_size("ctx") // 4
    paired = lax.axis_size("head") == 2 and width % (2 * CHUNK) == 0
    chunks = width // 2 // CHUNK if paired else 0
    quarter = (heads,) + states.shape[3:]
    vmem = pl.BlockSpec(memory_space=pltpu.VMEM)
    bf, f32 = jnp.bfloat16, jnp.float32
    dma = pltpu.SemaphoreType.DMA
    rows8 = (8, length)
    if paired:
        half = jax.ShapeDtypeStruct((width // 2, length), bf)
        outs = [half, half, jax.ShapeDtypeStruct(rows8, f32)]
        scratch = [
            pltpu.VMEM((2 * chunks, depth, CHUNK), bf),
            pltpu.VMEM((chunks, CHUNK, length), bf),
            pltpu.VMEM(rows8, f32),
            pltpu.VMEM(rows8, f32),
            pltpu.VMEM((length, hid), bf),
            dma((2 * chunks,)),
            dma((chunks,)),
            dma((chunks,)),
            dma((2,)),
        ]
    else:
        outs = [jax.ShapeDtypeStruct((length, hid), bf), jax.ShapeDtypeStruct(rows8, f32)]
        scratch = []
    scratch += [
        pltpu.VMEM((length, hid), bf),
        dma((1,)),
        pltpu.VMEM((length, hid), f32),
        pltpu.VMEM(states.shape, bf),
        pltpu.VMEM((2,) + quarter, bf),
        pltpu.VMEM(keep.shape, f32),
        pltpu.VMEM((2,) + quarter, bf),
        pltpu.VMEM(keep.shape, f32),
        pltpu.VMEM(quarter, bf),
        pltpu.VMEM(keep.shape, f32),
    ]
    scratch += [pltpu.VMEM(quarter, bf)] * 5
    scratch += [
        pltpu.VMEM((2,) + quarter, bf),
        dma((5, STEPS)),
        dma((5, STEPS)),
        dma((2,)),
        dma((2,)),
    ]
    result = pl.pallas_call(
        functools.partial(mixer_kernel, groups, chunks),
        out_shape=outs,
        in_specs=[vmem] * 7
        + [pl.BlockSpec(memory_space=pltpu.SMEM), vmem]
        + [pl.BlockSpec(memory_space=pl.ANY)] * 2,
        out_specs=[vmem] * len(outs),
        scratch_shapes=scratch,
        compiler_params=pltpu.CompilerParams(
            collective_id=0, has_side_effects=True, vmem_limit_bytes=44 * 1024 * 1024
        ),
    )(states, keep, xconv, scores, cum, delta, c_cols, skip, gain, z_in, w_out)
    if not paired:
        return project_any(result[0], result[1], w_out)
    own, got, inverse = result
    total = own.astype(f32) + got.astype(f32)
    return (total * inverse[:1]).astype(bf)


def rim_kernel(count, ranks, bc_ref, x_ref, all_ref, bct_ref, xt_ref, send, recv):
    idx = lax.axis_index("ctx")
    hd = lax.axis_index("head")
    has_prev = idx > 0
    has_next = idx < count - 1
    rows, length = bc_ref.shape
    lead = xt_ref.shape[0]
    barrier = pltpu.get_barrier_semaphore()

    def greet(place, shift):
        other = lax.rem(hd + shift, ranks)
        pl.semaphore_signal(barrier, inc=1, device_id=(place, other), device_id_type=MESH)

    for shift in range(1, ranks):
        greet(idx, shift)

    @pl.when(has_prev)
    def _():
        for shift in range(ranks):
            greet(idx - 1, shift)

    @pl.when(has_next)
    def _():
        for shift in range(ranks):
            greet(idx + 1, shift)

    mine = pl.ds(pl.multiple_of(hd * rows, rows), rows)
    all_ref[mine] = bc_ref[...]

    @pl.when(jnp.logical_not(has_prev))
    def _():
        bct_ref[...] = jnp.zeros_like(bct_ref)
        xt_ref[...] = jnp.zeros_like(xt_ref)

    neighbours = has_prev.astype(jnp.int32) + has_next.astype(jnp.int32)
    pl.semaphore_wait(barrier, ranks - 1 + ranks * neighbours)

    def copy(src, dst, kind, shift, place):
        return pltpu.make_async_remote_copy(
            src_ref=src, dst_ref=dst, send_sem=send.at[kind, shift], recv_sem=recv.at[kind, shift],
            device_id=(place, lax.rem(hd + shift, ranks)), device_id_type=MESH,
        )

    across = [copy(bc_ref, all_ref.at[mine], 0, k, idx) for k in range(1, ranks)]
    ahead = [copy(x_ref.at[pl.ds(x_ref.shape[0] - lead, lead)], xt_ref, 2, 0, idx + 1)]
    last = bc_ref.at[:, pl.ds(length - 128, 128)]
    ahead += [copy(last, bct_ref.at[mine], 1, k, idx + 1) for k in range(ranks)]

    @pl.when(has_next)
    def _():
        for cp in ahead:
            cp.start()

    for cp in across:
        cp.start()

    @pl.when(has_prev)
    def _():
        for cp in ahead:
            cp.wait_recv()

    for cp in across:
        cp.wait()

    @pl.when(has_next)
    def _():
        for cp in ahead:
            cp.wait_send()


def with_rims(bc_in, x_in):
    rows, length = bc_in.shape
    ranks = lax.axis_size("head")
    vmem = pl.BlockSpec(memory_space=pltpu.VMEM)
    dtype = bc_in.dtype
    return pl.pallas_call(
        functools.partial(rim_kernel, lax.axis_size("ctx"), ranks),
        out_shape=[
            jax.ShapeDtypeStruct((rows * ranks, length), dtype),
            jax.ShapeDtypeStruct((rows * ranks, 128), dtype),
            jax.ShapeDtypeStruct((16, x_in.shape[1]), dtype),
        ],
        in_specs=[vmem, pl.BlockSpec(memory_space=pl.ANY)],
        out_specs=[vmem] * 3,
        scratch_shapes=[pltpu.SemaphoreType.DMA((3, ranks)), pltpu.SemaphoreType.DMA((3, ranks))],
        compiler_params=pltpu.CompilerParams(
            collective_id=1, has_side_effects=True, vmem_limit_bytes=8 * 1024 * 1024
        ),
    )(bc_in, x_in)


def as_column(row):
    size = row.shape[0]
    rows = lax.broadcasted_iota(jnp.int32, (size, size), 0)
    cols = lax.broadcasted_iota(jnp.int32, (size, size), 1)
    return jnp.sum(jnp.where(rows == cols, row[None, :], 0.0), axis=1, keepdims=True)


def local_kernel(
    x_ref, xt_ref, bc_ref, bct_ref, dt_ref, bias_ref, rate_ref, cx_ref, cbc_ref,
    xc_ref, st_ref, keep_ref, score_ref, cum_ref, delta_ref, c_ref, b_s,
):
    f32, bf16 = jnp.float32, jnp.bfloat16
    step = pl.program_id(0)
    heads = dt_ref.shape[0]
    block = heads // STEPS
    length = x_ref.shape[0]

    @pl.when(step == 0)
    def _():
        lead = bct_ref.shape[1]
        wide = jnp.concatenate([bct_ref[...], bc_ref[...]], 1).astype(f32)
        summed = jnp.zeros(bc_ref.shape, f32)
        taps = jnp.concatenate([cbc_ref[...], jnp.zeros_like(cbc_ref)], 0).T
        for k in range(KCONV):
            first = lead - KCONV + 1 + k
            summed = summed + taps[:, k : k + 1] * wide[:, first : first + length]
        bcconv = silu(summed)
        b_s[...] = bcconv[:N].astype(bf16)
        c_ref[...] = bcconv[N:].astype(bf16)
        c_rows = bcconv[N:].T.astype(bf16)
        scores = jnp.dot(c_rows, b_s[...], preferred_element_type=f32)
        rows = lax.broadcasted_iota(jnp.int32, (length, length), 0)
        cols = lax.broadcasted_iota(jnp.int32, (length, length), 1)
        score_ref[...] = jnp.where(rows >= cols, scores, 0.0)
        raw = dt_ref[...] + as_column(bias_ref[...])
        delta = jnp.maximum(raw, 0.0) + jnp.log1p(jnp.exp(-jnp.abs(raw)))
        upper = jnp.where(rows <= cols, 1.0, 0.0)
        cum = jnp.dot(
            -delta * as_column(rate_ref[...]), upper,
            precision=lax.Precision.HIGHEST, preferred_element_type=f32,
        )
        keep_ref[...] = jnp.broadcast_to(jnp.exp(cum[:, length - 1 : length]), keep_ref.shape)
        for i in range(STEPS):
            part = slice(i * block, (i + 1) * block)
            cum_ref[i, 0:block] = cum[part]
            delta_ref[i, 0:block] = delta[part]

    lead = xt_ref.shape[0]
    cum8 = cum_ref[step]
    delta8 = delta_ref[step]
    tail8 = jnp.exp(cum8[:, length - 1 : length] - cum8) * delta8
    b_rows = b_s[...]
    for j in range(block // 2):
        lanes = slice(j * 128, (j + 1) * 128)
        wide = jnp.concatenate([xt_ref[:, lanes].astype(f32), x_ref[:, lanes].astype(f32)], 0)
        summed = jnp.zeros((length, 128), f32)
        for k in range(KCONV):
            first = lead - KCONV + 1 + k
            summed = summed + cx_ref[k : k + 1, lanes] * wide[first : first + length]
        pair = silu(summed).astype(bf16)
        xc_ref[:, lanes] = pair
        pair32 = pair.astype(f32)
        flipped = pair32.T
        for half in range(2):
            h = 2 * j + half
            scaled = (flipped[half * P_SIZE : (half + 1) * P_SIZE] * tail8[h : h + 1]).astype(bf16)
            state = lax.dot_general(
                scaled, b_rows, (((1,), (1,)), ((), ())), preferred_element_type=f32
            ).astype(bf16)
            for quarter in range(4):
                st_ref[quarter // 2, quarter % 2, h] = state[quarter * 16 : (quarter + 1) * 16]


def local_terms(x_in, x_tail, bc, bc_tail, dt_in, dt_bias, decay_rate, conv_x, conv_bc):
    length, width = x_in.shape
    heads = width // P_SIZE
    block = heads // STEPS
    cols = block * P_SIZE
    f32, bf16 = jnp.float32, jnp.bfloat16

    def whole(a):
        return pl.BlockSpec(a.shape, lambda i: (0,) * len(a.shape))

    def columns(rows):
        return pl.BlockSpec((rows, cols), lambda i: (0, i))

    args = (
        x_in, x_tail, bc, bc_tail, dt_in, dt_bias, decay_rate,
        conv_x, conv_bc.T,
    )
    in_specs = [columns(length), columns(x_tail.shape[0])] + [whole(a) for a in args[2:7]]
    in_specs += [columns(KCONV), whole(args[8])]
    outs = [
        jax.ShapeDtypeStruct((length, width), bf16),
        jax.ShapeDtypeStruct((2, 2, heads, P_SIZE // 4, N), bf16),
        jax.ShapeDtypeStruct((heads, N), f32),
        jax.ShapeDtypeStruct((length, length), f32),
        jax.ShapeDtypeStruct((STEPS, 8, length), f32),
        jax.ShapeDtypeStruct((STEPS, 8, length), f32),
        jax.ShapeDtypeStruct((N, length), bf16),
    ]
    out_specs = [
        columns(length),
        pl.BlockSpec((2, 2, block, P_SIZE // 4, N), lambda i: (0, 0, i, 0, 0)),
    ] + [whole(a) for a in outs[2:]]
    return pl.pallas_call(
        local_kernel,
        out_shape=outs,
        grid=(STEPS,),
        in_specs=in_specs,
        out_specs=out_specs,
        scratch_shapes=[
            pltpu.VMEM((N, length), bf16),
        ],
        compiler_params=pltpu.CompilerParams(vmem_limit_bytes=32 * 1024 * 1024),
    )(*args)


def project_any(hidden, squares, w_out):
    inverse = lax.rsqrt(lax.psum(squares[0], "head") / (HEADS * P_SIZE) + EPSILON)
    ranks = lax.axis_size("head")
    rank = lax.axis_index("head")
    share = w_out.shape[1] // ranks

    def project(owner):
        rows = lax.dynamic_slice_in_dim(w_out, owner * share, share, 1)
        return lax.dot_general(
            rows, hidden, (((0,), (1,)), ((), ())), preferred_element_type=jnp.float32
        ).astype(jnp.bfloat16)

    arrived = []
    for shift in range(1, ranks):
        piece = project(lax.rem(rank + shift, ranks))
        arrived.append(
            lax.ppermute(piece, "head", [(i, (i + shift) % ranks) for i in range(ranks)])
        )
    total = project(rank).astype(jnp.float32)
    for piece in arrived:
        total = total + piece.astype(jnp.float32)
    return (total * inverse[None, :]).astype(jnp.bfloat16)


def on_device(
    x_in, z_in, bc_in, dt_in, dt_bias, decay_rate, d_skip, conv_x, conv_bc, norm_gain, w_out
):
    bc, bc_tail, x_tail = with_rims(bc_in, x_in)
    terms = local_terms(
        x_in, x_tail, bc, bc_tail, dt_in, dt_bias, decay_rate, conv_x, conv_bc
    )
    xconv, states, keep, scores, cum, delta, c_cols = terms
    return mix(
        states, keep, xconv, scores, cum, delta, c_cols, d_skip, norm_gain, z_in, w_out
    )


def solution(mesh):
    in_specs = (
        P("ctx", "head"),
        P("ctx", "head"),
        P("head", "ctx"),
        P("head", "ctx"),
        P("head"),
        P("head"),
        P("head"),
        P(None, "head"),
        P(),
        P("head"),
        P("head", None),
    )
    out_specs = P("head", "ctx")
    return jax.shard_map(
        on_device, mesh=mesh, in_specs=in_specs, out_specs=out_specs, check_vma=False
    )
```

```python
import functools

import jax
import jax.numpy as jnp
from jax import lax
from jax.experimental import pallas as pl
from jax.experimental.pallas import tpu as pltpu
from jax.sharding import PartitionSpec as P

HEADS = 80
N = 128
P_SIZE = 64
KCONV = 4
SPAN = 256


EPSILON = 1e-05
MESH = pl.DeviceIdType.MESH


STEPS = 5
CHUNK = 256


def silu(v):
    return v / (1.0 + jnp.exp(-v))


def as_column(row):
    size = row.shape[0]
    rows = lax.broadcasted_iota(jnp.int32, (size, size), 0)
    cols = lax.broadcasted_iota(jnp.int32, (size, size), 1)
    return jnp.sum(jnp.where(rows == cols, row[None, :], 0.0), axis=1, keepdims=True)


def mixer_kernel(
    count, ranks, chunks, bc_ref, dt_ref, bias_ref, rate_ref, cx_ref, cbc_ref, skip_ref, gain_ref,
    x_ref, z_ref, w_ref, *rest,
):
    if chunks:
        own_ref, got_ref, inv_ref, *rest = rest
        w_s, send_s, sq_s, sq_own, hid_s, load, psend, precv, sq_sem, *rest = rest
    else:
        hid_s, sq_own, *rest = rest
    (
        s_ref, k_ref, xc_ref, score_ref, cum_ref, delta_ref, c_ref, b_ref,
        x_s, all_ref, bct_ref, xt_ref, rsend, rrecv,
        z_s, z_sem, y_s, e_s, ra, rka, tb, ktb, rb, rkb, sc, rc, sd, rd, oe, se,
        send, recv, ksend, krecv,
    ) = rest
    f32, bf16 = jnp.float32, jnp.bfloat16
    idx = lax.axis_index("ctx")
    hd = lax.axis_index("head")
    c = lax.rem(idx, 2)
    x = lax.rem(lax.div(idx, 2), 2)
    g = lax.div(idx, 4)
    core_peer = idx + 1 - 2 * c
    x_peer = idx + 2 - 4 * x
    groups = count // 4
    has_prev = g > 0
    has_next = g < groups - 1
    has_left = idx > 0
    has_right = idx < count - 1
    heads = k_ref.shape[0]
    size = heads // STEPS
    cols = size * P_SIZE
    length = xc_ref.shape[0]
    x_load = pltpu.make_async_copy(x_ref, x_s, z_sem.at[1])
    x_load.start()

    barrier = pltpu.get_barrier_semaphore()

    def greet(place, shift):
        other = lax.rem(hd + shift, ranks)
        pl.semaphore_signal(barrier, inc=1, device_id=(place, other), device_id_type=MESH)

    greet(x_peer, 0)
    for shift in range(1, ranks):
        greet(idx, shift)

    @pl.when(has_left)
    def _():
        for shift in range(ranks):
            greet(idx - 1, shift)

    @pl.when(has_right)
    def _():
        for shift in range(ranks):
            greet(idx + 1, shift)

    @pl.when(has_prev)
    def _():
        greet(idx - 4, 0)

    @pl.when(has_next)
    def _():
        greet(idx + 4, 0)

    def flag(value):
        return value.astype(jnp.int32)

    rows = bc_ref.shape[0]
    lead = xt_ref.shape[0]
    mine_rows = pl.ds(pl.multiple_of(hd * rows, rows), rows)
    all_ref[mine_rows] = bc_ref[...]

    @pl.when(jnp.logical_not(has_left))
    def _():
        bct_ref[...] = jnp.zeros_like(bct_ref)
        xt_ref[...] = jnp.zeros_like(xt_ref)

    pl.semaphore_wait(
        barrier,
        ranks + ranks * (flag(has_left) + flag(has_right)) + flag(has_prev) + flag(has_next),
    )

    def rim_copy(src, dst, kind, shift, place):
        return pltpu.make_async_remote_copy(
            src_ref=src, dst_ref=dst, send_sem=rsend.at[kind, shift], recv_sem=rrecv.at[kind, shift],
            device_id=(place, lax.rem(hd + shift, ranks)), device_id_type=MESH,
        )

    across = [rim_copy(bc_ref, all_ref.at[mine_rows], 0, k, idx) for k in range(1, ranks)]
    tail_rows = x_ref.at[pl.ds(length - lead, lead)]
    ahead = [rim_copy(tail_rows, xt_ref, 2, 0, idx + 1)]
    last = bc_ref.at[:, pl.ds(length - 128, 128)]
    ahead += [rim_copy(last, bct_ref.at[mine_rows], 1, k, idx + 1) for k in range(ranks)]

    @pl.when(has_right)
    def _():
        for cp in ahead:
            cp.start()

    for cp in across:
        cp.start()

    z_load = pltpu.make_async_copy(z_ref, z_s, z_sem.at[0])
    z_load.start()
    loads = []
    for i in range(2 * chunks):
        base = (1 - hd if i < chunks else hd) * (chunks * CHUNK) + (i % chunks) * CHUNK
        base = pl.multiple_of(base, CHUNK)
        cp = pltpu.make_async_copy(w_ref.at[:, pl.ds(base, CHUNK)], w_s.at[i], load.at[i])
        cp.start()
        loads.append(cp)

    row_ids = lax.broadcasted_iota(jnp.int32, (length, length), 0)
    col_ids = lax.broadcasted_iota(jnp.int32, (length, length), 1)
    raw = dt_ref[...] + as_column(bias_ref[...])
    delta = jnp.maximum(raw, 0.0) + jnp.log1p(jnp.exp(-jnp.abs(raw)))
    cum = jnp.dot(
        -delta * as_column(rate_ref[...]), jnp.where(row_ids <= col_ids, 1.0, 0.0),
        precision=lax.Precision.HIGHEST, preferred_element_type=f32,
    )
    k_ref[...] = jnp.broadcast_to(jnp.exp(cum[:, length - 1 : length]), k_ref.shape)
    for i in range(STEPS):
        cum_ref[i, 0:size] = cum[i * size : (i + 1) * size]
        delta_ref[i, 0:size] = delta[i * size : (i + 1) * size]

    def copy(src, dst, phase, j, dev):
        return pltpu.make_async_remote_copy(
            src_ref=src, dst_ref=dst, send_sem=send.at[phase, j], recv_sem=recv.at[phase, j],
            device_id=(dev, hd), device_id_type=MESH,
        )

    def keep_copy(src, dst, j, dev):
        return pltpu.make_async_remote_copy(
            src_ref=src, dst_ref=dst, send_sem=ksend.at[j], recv_sem=krecv.at[j],
            device_id=(dev, hd), device_id_type=MESH,
        )

    part = [pl.ds(j * size, size) for j in range(STEPS)]
    ka = keep_copy(k_ref, rka, 0, core_peer)
    ka.start()
    step_a = [copy(s_ref.at[1 - c, :, d], ra.at[:, d], 0, j, core_peer) for j, d in enumerate(part)]

    @pl.when(has_left)
    def _():
        for cp in ahead:
            cp.wait_recv()

    for cp in across:
        cp.wait_recv()
    taps = jnp.concatenate([cbc_ref[...], jnp.zeros_like(cbc_ref)], 0).T
    wide = jnp.concatenate([bct_ref[...], all_ref[...]], 1).astype(f32)
    summed = jnp.zeros(all_ref.shape, f32)
    for k in range(KCONV):
        first = 128 - KCONV + 1 + k
        summed = summed + taps[:, k : k + 1] * wide[:, first : first + length]
    bcconv = silu(summed)
    b_ref[...] = bcconv[:N].astype(bf16)
    c_ref[...] = bcconv[N:].astype(bf16)
    scores = jnp.dot(bcconv[N:].T.astype(bf16), b_ref[...], preferred_element_type=f32)
    score_ref[...] = jnp.where(row_ids >= col_ids, scores, 0.0)
    b_rows = b_ref[...]
    x_load.wait()
    for i in range(STEPS):
        cum8 = cum_ref[i]
        tail8 = jnp.exp(cum8[:, length - 1 : length] - cum8) * delta_ref[i]
        for j in range(size // 2):
            lanes = slice(i * cols + j * 128, i * cols + (j + 1) * 128)
            wide = jnp.concatenate([xt_ref[:, lanes].astype(f32), x_s[:, lanes].astype(f32)], 0)
            summed = jnp.zeros((length, 128), f32)
            for k in range(KCONV):
                first = lead - KCONV + 1 + k
                summed = summed + cx_ref[k : k + 1, lanes] * wide[first : first + length]
            pair = silu(summed).astype(bf16)
            xc_ref[:, lanes] = pair
            flipped = pair.astype(f32).T
            for half in range(2):
                h = 2 * j + half
                scaled = flipped[half * P_SIZE : (half + 1) * P_SIZE] * tail8[h : h + 1]
                state = lax.dot_general(
                    scaled.astype(bf16), b_rows, (((1,), (1,)), ((), ())),
                    preferred_element_type=f32,
                ).astype(bf16)
                for q in range(4):
                    s_ref[q // 2, q % 2, i * size + h] = state[q * 16 : (q + 1) * 16]
        step_a[i].start()

    @pl.when(jnp.logical_not(has_prev))
    def _():
        rc[...] = jnp.zeros_like(rc)

    def local_chunks(low, high):
        @pl.loop(low, high)
        def _(i):
            cum8 = cum_ref[i]
            delta8 = delta_ref[i]
            cum_cols = cum8.T
            scores = score_ref[...]
            left = lax.broadcasted_iota(jnp.int32, (length, 128), 1) < P_SIZE
            for j in range(size // 2):
                lanes = pl.ds(pl.multiple_of(i * cols + j * 128, 128), 128)
                pair = xc_ref[:, lanes].astype(f32)
                weights = []
                for h in (2 * j, 2 * j + 1):
                    gap = jnp.minimum(cum_cols[:, h : h + 1] - cum8[h : h + 1], 0.0)
                    weights.append((scores * jnp.exp(gap) * delta8[h : h + 1]).astype(bf16))
                both = jnp.concatenate(
                    [jnp.where(left, pair, 0.0), jnp.where(left, 0.0, pair)], 0
                ).astype(bf16)
                local = jnp.dot(jnp.concatenate(weights, 1), both, preferred_element_type=f32)
                first = i * size + 2 * j
                y_s[:, lanes] = local + jnp.where(left, skip_ref[first], skip_ref[first + 1]) * pair

    early = jnp.minimum(2 + g, STEPS)
    local_chunks(0, 1)

    ka.wait_recv()
    ktb[...] = k_ref[...] * rka[...]
    kb = keep_copy(ktb, rkb, 1, x_peer)
    kb.start()
    is_core0 = c == 0
    is_x0 = x == 0

    step_b = [copy(tb.at[1 - x, d], rb.at[d], 1, j, x_peer) for j, d in enumerate(part)]
    for j, d in enumerate(part):
        step_a[j].wait_recv()
        own = s_ref[c, :, d].astype(f32)
        peer = ra[:, d].astype(f32)
        first = jnp.where(is_core0, own, peer)
        second = jnp.where(is_core0, peer, own)
        keep = jnp.where(is_core0, rka[d], k_ref[d])
        tb[:, d] = (keep[None, :, None, :] * first + second).astype(bf16)
        step_b[j].start()

    local_chunks(1, early)

    kb.wait_recv()
    step_c = [copy(sc.at[d], rc.at[d], 2, j, idx + 4) for j, d in enumerate(part)]
    step_d = [copy(sd.at[d], rd.at[d], 3, j, x_peer) for j, d in enumerate(part)]
    for j, d in enumerate(part):
        step_b[j].wait_recv()
        own = tb[x, d].astype(f32)
        peer = rb[d].astype(f32)
        first = jnp.where(is_x0, own, peer)
        second = jnp.where(is_x0, peer, own)
        keep0 = jnp.where(is_x0, ktb[d], rkb[d])[:, None, :]
        keep1 = jnp.where(is_x0, rkb[d], ktb[d])[:, None, :]

        @pl.when(has_prev)
        def _():
            step_c[j].wait_recv()

        entry = rc[d].astype(f32)
        after = keep0 * entry + first

        @pl.when(has_next)
        def _():
            sc[d] = (keep1 * after + second).astype(bf16)
            step_c[j].start()

        sd[d] = jnp.where(is_x0, after, entry).astype(bf16)
        step_d[j].start()
        oe[d] = jnp.where(is_x0, entry, after).astype(bf16)

    local_chunks(early, STEPS)
    z_load.wait()

    step_e = [copy(se.at[:, d], e_s.at[c, :, d], 4, j, core_peer) for j, d in enumerate(part)]
    squares = jnp.zeros((length, 128), f32)
    c_cols = c_ref[...]
    for j in range(STEPS + 1):
        if j < STEPS:
            d = part[j]
            step_d[j].wait_recv()
            keep = jnp.where(is_core0, k_ref[d], rka[d])[:, None, :]
            for quarter, source in ((x, oe), (1 - x, rd)):
                entry = source[d].astype(f32)
                mine = jnp.where(
                    is_core0, s_ref[c, quarter, d].astype(f32), ra[quarter, d].astype(f32)
                )
                after = keep * entry + mine
                e_s[c, quarter, d] = jnp.where(is_core0, entry, after).astype(bf16)
                se[quarter, d] = jnp.where(is_core0, after, entry).astype(bf16)
            step_e[j].start()
        if j > 0:
            i = j - 1
            step_e[i].wait_recv()
            grown = jnp.exp(cum_ref[i])
            for n in range(size // 2):
                lanes = slice(i * cols + n * 128, i * cols + (n + 1) * 128)
                entry = jnp.concatenate(
                    [
                        e_s[q // 2, q % 2, i * size + h]
                        for h in (2 * n, 2 * n + 1)
                        for q in range(4)
                    ],
                    0,
                )
                carried = jnp.dot(entry, c_cols, preferred_element_type=f32)
                carried = jnp.concatenate(
                    [
                        carried[:P_SIZE] * grown[2 * n : 2 * n + 1],
                        carried[P_SIZE:] * grown[2 * n + 1 : 2 * n + 2],
                    ],
                    0,
                ).T
                gated = (y_s[:, lanes] + carried) * silu(z_s[:, lanes].astype(f32))
                squares = squares + gated * gated
                hid_s[:, lanes] = (gated * gain_ref[lanes][None, :]).astype(bf16)

    sq_own[...] = lax.dot_general(
        jnp.ones((8, 128), f32), squares, (((1,), (1,)), ((), ())),
        precision=lax.Precision.HIGHEST, preferred_element_type=f32,
    )
    if chunks:
        sq_copy = pltpu.make_async_remote_copy(
            src_ref=sq_own, dst_ref=sq_s, send_sem=sq_sem.at[0], recv_sem=sq_sem.at[1],
            device_id=(idx, 1 - hd), device_id_type=MESH,
        )
        sq_copy.start()
        copies = []
        for i in range(2 * chunks):
            loads[i].wait()
            flipped = jnp.dot(hid_s[...], w_s[i], preferred_element_type=f32).T.astype(bf16)
            j = i % chunks
            rows = pl.ds(j * CHUNK, CHUNK)
            if i < chunks:
                send_s[j] = flipped
                cp = pltpu.make_async_remote_copy(
                    src_ref=send_s.at[j], dst_ref=got_ref.at[rows],
                    send_sem=psend.at[j], recv_sem=precv.at[j],
                    device_id=(idx, 1 - hd), device_id_type=MESH,
                )
                cp.start()
                copies.append(cp)
            else:
                own_ref[rows] = flipped
        sq_copy.wait()
        inv_ref[...] = lax.rsqrt((sq_own[...] + sq_s[...]) / (HEADS * P_SIZE) + EPSILON)
        for cp in copies:
            cp.wait()

    for cp in across:
        cp.wait_send()

    @pl.when(has_right)
    def _():
        for cp in ahead:
            cp.wait_send()

    ka.wait_send()
    kb.wait_send()
    for j in range(STEPS):
        step_a[j].wait_send()
        step_b[j].wait_send()
        step_d[j].wait_send()
        step_e[j].wait_send()

    @pl.when(has_next)
    def _():
        for cp in step_c:
            cp.wait_send()


def on_device(
    x_in, z_in, bc_in, dt_in, dt_bias, decay_rate, d_skip, conv_x, conv_bc, norm_gain, w_out
):
    length, hid = x_in.shape
    heads = hid // P_SIZE
    states = jax.ShapeDtypeStruct((2, 2, heads, P_SIZE // 4, N), jnp.bfloat16)
    keep = jax.ShapeDtypeStruct((heads, N), jnp.float32)
    count = lax.axis_size("ctx")
    ranks = lax.axis_size("head")
    depth, width = w_out.shape
    paired = ranks == 2 and width % (2 * CHUNK) == 0
    chunks = width // 2 // CHUNK if paired else 0
    quarter = (heads,) + states.shape[3:]
    vmem = pl.BlockSpec(memory_space=pltpu.VMEM)
    bf, f32 = jnp.bfloat16, jnp.float32
    dma = pltpu.SemaphoreType.DMA
    rows8 = (8, length)
    if paired:
        half = jax.ShapeDtypeStruct((width // 2, length), bf)
        outs = [half, half, jax.ShapeDtypeStruct(rows8, f32)]
        scratch = [
            pltpu.VMEM((2 * chunks, depth, CHUNK), bf),
            pltpu.VMEM((chunks, CHUNK, length), bf),
            pltpu.VMEM(rows8, f32),
            pltpu.VMEM(rows8, f32),
            pltpu.VMEM((length, hid), bf),
            dma((2 * chunks,)),
            dma((chunks,)),
            dma((chunks,)),
            dma((2,)),
        ]
    else:
        outs = [jax.ShapeDtypeStruct((length, hid), bf), jax.ShapeDtypeStruct(rows8, f32)]
        scratch = []
    scratch += [
        pltpu.VMEM(states.shape, bf),
        pltpu.VMEM(keep.shape, f32),
        pltpu.VMEM((length, hid), bf),
        pltpu.VMEM((length, length), f32),
        pltpu.VMEM((STEPS,) + rows8, f32),
        pltpu.VMEM((STEPS,) + rows8, f32),
        pltpu.VMEM((N, length), bf),
        pltpu.VMEM((N, length), bf),
        pltpu.VMEM((length, hid), bf),
        pltpu.VMEM((2 * N, length), bf),
        pltpu.VMEM((2 * N, 128), bf),
        pltpu.VMEM((16, hid), bf),
        dma((3, ranks)),
        dma((3, ranks)),
        pltpu.VMEM((length, hid), bf),
        dma((2,)),
        pltpu.VMEM((length, hid), f32),
        pltpu.VMEM(states.shape, bf),
        pltpu.VMEM((2,) + quarter, bf),
        pltpu.VMEM(keep.shape, f32),
        pltpu.VMEM((2,) + quarter, bf),
        pltpu.VMEM(keep.shape, f32),
        pltpu.VMEM(quarter, bf),
        pltpu.VMEM(keep.shape, f32),
    ]
    scratch += [pltpu.VMEM(quarter, bf)] * 5
    scratch += [
        pltpu.VMEM((2,) + quarter, bf),
        dma((5, STEPS)),
        dma((5, STEPS)),
        dma((2,)),
        dma((2,)),
    ]
    result = pl.pallas_call(
        functools.partial(mixer_kernel, count, ranks, chunks),
        out_shape=outs,
        in_specs=[vmem] * 6
        + [pl.BlockSpec(memory_space=pltpu.SMEM), vmem]
        + [pl.BlockSpec(memory_space=pl.ANY)] * 3,
        out_specs=[vmem] * len(outs),
        scratch_shapes=scratch,
        compiler_params=pltpu.CompilerParams(
            collective_id=0, has_side_effects=True, vmem_limit_bytes=60 * 1024 * 1024
        ),
    )(
        bc_in, dt_in, dt_bias, decay_rate, conv_x, conv_bc.T, d_skip, norm_gain,
        x_in, z_in, w_out,
    )
    if not paired:
        return project_any(result[0], result[1], w_out)
    own, got, inverse = result
    total = own.astype(f32) + got.astype(f32)
    return (total * inverse[:1]).astype(bf)


def project_any(hidden, squares, w_out):
    inverse = lax.rsqrt(lax.psum(squares[0], "head") / (HEADS * P_SIZE) + EPSILON)
    ranks = lax.axis_size("head")
    rank = lax.axis_index("head")
    share = w_out.shape[1] // ranks

    def project(owner):
        rows = lax.dynamic_slice_in_dim(w_out, owner * share, share, 1)
        return lax.dot_general(
            rows, hidden, (((0,), (1,)), ((), ())), preferred_element_type=jnp.float32
        ).astype(jnp.bfloat16)

    arrived = []
    for shift in range(1, ranks):
        piece = project(lax.rem(rank + shift, ranks))
        arrived.append(
            lax.ppermute(piece, "head", [(i, (i + shift) % ranks) for i in range(ranks)])
        )
    total = project(rank).astype(jnp.float32)
    for piece in arrived:
        total = total + piece.astype(jnp.float32)
    return (total * inverse[None, :]).astype(jnp.bfloat16)


def solution(mesh):
    in_specs = (
        P("ctx", "head"),
        P("ctx", "head"),
        P("head", "ctx"),
        P("head", "ctx"),
        P("head"),
        P("head"),
        P("head"),
        P(None, "head"),
        P(),
        P("head"),
        P("head", None),
    )
    out_specs = P("head", "ctx")
    return jax.shard_map(
        on_device, mesh=mesh, in_specs=in_specs, out_specs=out_specs, check_vma=False
    )
```

```python
import functools

import jax
import jax.numpy as jnp
from jax import lax
from jax.experimental import pallas as pl
from jax.experimental.pallas import tpu as pltpu
from jax.sharding import PartitionSpec as P

HEADS = 80
N = 128
P_SIZE = 64
KCONV = 4
SPAN = 256


EPSILON = 1e-05
MESH = pl.DeviceIdType.MESH


STEPS = 5
CHUNK = 256


def silu(v):
    return v / (1.0 + jnp.exp(-v))


def as_column(row):
    size = row.shape[0]
    rows = lax.broadcasted_iota(jnp.int32, (size, size), 0)
    cols = lax.broadcasted_iota(jnp.int32, (size, size), 1)
    return jnp.sum(jnp.where(rows == cols, row[None, :], 0.0), axis=1, keepdims=True)


def mixer_kernel(
    count, ranks, chunks, bc_ref, dt_ref, bias_ref, rate_ref, cx_ref, cbc_ref, skip_ref, gain_ref,
    x_ref, z_ref, w_ref, *rest,
):
    if chunks:
        out_ref, *rest = rest
        w_s, got_s, send_s, sq_s, sq_own, hid_s, load, psend, precv, sq_sem, *rest = rest
    else:
        hid_s, sq_own, *rest = rest
    (
        s_ref, k_ref, xc_ref, score_ref, cum_ref, delta_ref, c_ref, b_ref,
        x_s, all_ref, bct_ref, xt_ref, rsend, rrecv,
        z_s, z_sem, y_s, e_s, ra, rka, tb, ktb, rb, rkb, sc, rc, sd, rd, oe, se,
        send, recv, ksend, krecv,
    ) = rest
    f32, bf16 = jnp.float32, jnp.bfloat16
    idx = lax.axis_index("ctx")
    hd = lax.axis_index("head")
    c = lax.rem(idx, 2)
    x = lax.rem(lax.div(idx, 2), 2)
    g = lax.div(idx, 4)
    core_peer = idx + 1 - 2 * c
    x_peer = idx + 2 - 4 * x
    groups = count // 4
    has_prev = g > 0
    has_next = g < groups - 1
    has_left = idx > 0
    has_right = idx < count - 1
    heads = k_ref.shape[0]
    size = heads // STEPS
    cols = size * P_SIZE
    length = xc_ref.shape[0]
    x_load = pltpu.make_async_copy(x_ref, x_s, z_sem.at[1])
    x_load.start()

    barrier = pltpu.get_barrier_semaphore()

    def greet(place, shift):
        other = lax.rem(hd + shift, ranks)
        pl.semaphore_signal(barrier, inc=1, device_id=(place, other), device_id_type=MESH)

    greet(x_peer, 0)
    for shift in range(1, ranks):
        greet(idx, shift)

    @pl.when(has_left)
    def _():
        for shift in range(ranks):
            greet(idx - 1, shift)

    @pl.when(has_right)
    def _():
        for shift in range(ranks):
            greet(idx + 1, shift)

    @pl.when(has_prev)
    def _():
        greet(idx - 4, 0)

    @pl.when(has_next)
    def _():
        greet(idx + 4, 0)

    def flag(value):
        return value.astype(jnp.int32)

    rows = bc_ref.shape[0]
    lead = xt_ref.shape[0]
    mine_rows = pl.ds(pl.multiple_of(hd * rows, rows), rows)
    all_ref[mine_rows] = bc_ref[...]

    @pl.when(jnp.logical_not(has_left))
    def _():
        bct_ref[...] = jnp.zeros_like(bct_ref)
        xt_ref[...] = jnp.zeros_like(xt_ref)

    pl.semaphore_wait(
        barrier,
        ranks + ranks * (flag(has_left) + flag(has_right)) + flag(has_prev) + flag(has_next),
    )

    def rim_copy(src, dst, kind, shift, place):
        return pltpu.make_async_remote_copy(
            src_ref=src, dst_ref=dst, send_sem=rsend.at[kind, shift], recv_sem=rrecv.at[kind, shift],
            device_id=(place, lax.rem(hd + shift, ranks)), device_id_type=MESH,
        )

    across = [rim_copy(bc_ref, all_ref.at[mine_rows], 0, k, idx) for k in range(1, ranks)]
    tail_rows = x_ref.at[pl.ds(length - lead, lead)]
    ahead = [rim_copy(tail_rows, xt_ref, 2, 0, idx + 1)]
    last = bc_ref.at[:, pl.ds(length - 128, 128)]
    ahead += [rim_copy(last, bct_ref.at[mine_rows], 1, k, idx + 1) for k in range(ranks)]

    @pl.when(has_right)
    def _():
        for cp in ahead:
            cp.start()

    for cp in across:
        cp.start()

    z_load = pltpu.make_async_copy(z_ref, z_s, z_sem.at[0])
    z_load.start()
    loads = []
    for i in range(2 * chunks):
        base = (1 - hd if i < chunks else hd) * (chunks * CHUNK) + (i % chunks) * CHUNK
        base = pl.multiple_of(base, CHUNK)
        cp = pltpu.make_async_copy(w_ref.at[:, pl.ds(base, CHUNK)], w_s.at[i], load.at[i])
        cp.start()
        loads.append(cp)

    row_ids = lax.broadcasted_iota(jnp.int32, (length, length), 0)
    col_ids = lax.broadcasted_iota(jnp.int32, (length, length), 1)
    raw = dt_ref[...] + as_column(bias_ref[...])
    delta = jnp.maximum(raw, 0.0) + jnp.log1p(jnp.exp(-jnp.abs(raw)))
    cum = jnp.dot(
        -delta * as_column(rate_ref[...]), jnp.where(row_ids <= col_ids, 1.0, 0.0),
        precision=lax.Precision.HIGHEST, preferred_element_type=f32,
    )
    k_ref[...] = jnp.broadcast_to(jnp.exp(cum[:, length - 1 : length]), k_ref.shape)
    for i in range(STEPS):
        cum_ref[i, 0:size] = cum[i * size : (i + 1) * size]
        delta_ref[i, 0:size] = delta[i * size : (i + 1) * size]

    def copy(src, dst, phase, j, dev):
        return pltpu.make_async_remote_copy(
            src_ref=src, dst_ref=dst, send_sem=send.at[phase, j], recv_sem=recv.at[phase, j],
            device_id=(dev, hd), device_id_type=MESH,
        )

    def keep_copy(src, dst, j, dev):
        return pltpu.make_async_remote_copy(
            src_ref=src, dst_ref=dst, send_sem=ksend.at[j], recv_sem=krecv.at[j],
            device_id=(dev, hd), device_id_type=MESH,
        )

    part = [pl.ds(j * size, size) for j in range(STEPS)]
    ka = keep_copy(k_ref, rka, 0, core_peer)
    ka.start()
    step_a = [copy(s_ref.at[1 - c, :, d], ra.at[:, d], 0, j, core_peer) for j, d in enumerate(part)]

    @pl.when(has_left)
    def _():
        for cp in ahead:
            cp.wait_recv()

    for cp in across:
        cp.wait_recv()
    taps = jnp.concatenate([cbc_ref[...], jnp.zeros_like(cbc_ref)], 0).T
    wide = jnp.concatenate([bct_ref[...], all_ref[...]], 1).astype(f32)
    summed = jnp.zeros(all_ref.shape, f32)
    for k in range(KCONV):
        first = 128 - KCONV + 1 + k
        summed = summed + taps[:, k : k + 1] * wide[:, first : first + length]
    bcconv = silu(summed)
    b_ref[...] = bcconv[:N].astype(bf16)
    c_ref[...] = bcconv[N:].astype(bf16)
    scores = jnp.dot(bcconv[N:].T.astype(bf16), b_ref[...], preferred_element_type=f32)
    score_ref[...] = jnp.where(row_ids >= col_ids, scores, 0.0)
    b_rows = b_ref[...]
    x_load.wait()
    for i in range(STEPS):
        cum8 = cum_ref[i]
        tail8 = jnp.exp(cum8[:, length - 1 : length] - cum8) * delta_ref[i]
        for j in range(size // 2):
            lanes = slice(i * cols + j * 128, i * cols + (j + 1) * 128)
            wide = jnp.concatenate([xt_ref[:, lanes].astype(f32), x_s[:, lanes].astype(f32)], 0)
            summed = jnp.zeros((length, 128), f32)
            for k in range(KCONV):
                first = lead - KCONV + 1 + k
                summed = summed + cx_ref[k : k + 1, lanes] * wide[first : first + length]
            pair = silu(summed).astype(bf16)
            xc_ref[:, lanes] = pair
            flipped = pair.astype(f32).T
            for half in range(2):
                h = 2 * j + half
                scaled = flipped[half * P_SIZE : (half + 1) * P_SIZE] * tail8[h : h + 1]
                state = lax.dot_general(
                    scaled.astype(bf16), b_rows, (((1,), (1,)), ((), ())),
                    preferred_element_type=f32,
                ).astype(bf16)
                for q in range(4):
                    s_ref[q // 2, q % 2, i * size + h] = state[q * 16 : (q + 1) * 16]
        step_a[i].start()

    @pl.when(jnp.logical_not(has_prev))
    def _():
        rc[...] = jnp.zeros_like(rc)

    def local_chunks(low, high):
        @pl.loop(low, high)
        def _(i):
            cum8 = cum_ref[i]
            delta8 = delta_ref[i]
            cum_cols = cum8.T
            scores = score_ref[...]
            left = lax.broadcasted_iota(jnp.int32, (length, 128), 1) < P_SIZE
            for j in range(size // 2):
                lanes = pl.ds(pl.multiple_of(i * cols + j * 128, 128), 128)
                pair = xc_ref[:, lanes].astype(f32)
                weights = []
                for h in (2 * j, 2 * j + 1):
                    gap = jnp.minimum(cum_cols[:, h : h + 1] - cum8[h : h + 1], 0.0)
                    weights.append((scores * jnp.exp(gap) * delta8[h : h + 1]).astype(bf16))
                both = jnp.concatenate(
                    [jnp.where(left, pair, 0.0), jnp.where(left, 0.0, pair)], 0
                ).astype(bf16)
                local = jnp.dot(jnp.concatenate(weights, 1), both, preferred_element_type=f32)
                first = i * size + 2 * j
                y_s[:, lanes] = local + jnp.where(left, skip_ref[first], skip_ref[first + 1]) * pair

    early = jnp.minimum(2 + g, STEPS)
    local_chunks(0, 1)

    ka.wait_recv()
    ktb[...] = k_ref[...] * rka[...]
    kb = keep_copy(ktb, rkb, 1, x_peer)
    kb.start()
    is_core0 = c == 0
    is_x0 = x == 0

    step_b = [copy(tb.at[1 - x, d], rb.at[d], 1, j, x_peer) for j, d in enumerate(part)]
    for j, d in enumerate(part):
        step_a[j].wait_recv()
        own = s_ref[c, :, d].astype(f32)
        peer = ra[:, d].astype(f32)
        first = jnp.where(is_core0, own, peer)
        second = jnp.where(is_core0, peer, own)
        keep = jnp.where(is_core0, rka[d], k_ref[d])
        tb[:, d] = (keep[None, :, None, :] * first + second).astype(bf16)
        step_b[j].start()

    local_chunks(1, early)

    kb.wait_recv()
    step_c = [copy(sc.at[d], rc.at[d], 2, j, idx + 4) for j, d in enumerate(part)]
    step_d = [copy(sd.at[d], rd.at[d], 3, j, x_peer) for j, d in enumerate(part)]
    for j, d in enumerate(part):
        step_b[j].wait_recv()
        own = tb[x, d].astype(f32)
        peer = rb[d].astype(f32)
        first = jnp.where(is_x0, own, peer)
        second = jnp.where(is_x0, peer, own)
        keep0 = jnp.where(is_x0, ktb[d], rkb[d])[:, None, :]
        keep1 = jnp.where(is_x0, rkb[d], ktb[d])[:, None, :]

        @pl.when(has_prev)
        def _():
            step_c[j].wait_recv()

        entry = rc[d].astype(f32)
        after = keep0 * entry + first

        @pl.when(has_next)
        def _():
            sc[d] = (keep1 * after + second).astype(bf16)
            step_c[j].start()

        sd[d] = jnp.where(is_x0, after, entry).astype(bf16)
        step_d[j].start()
        oe[d] = jnp.where(is_x0, entry, after).astype(bf16)

    local_chunks(early, STEPS)
    z_load.wait()

    step_e = [copy(se.at[:, d], e_s.at[c, :, d], 4, j, core_peer) for j, d in enumerate(part)]
    squares = jnp.zeros((length, 128), f32)
    c_cols = c_ref[...]
    for j in range(STEPS + 1):
        if j < STEPS:
            d = part[j]
            step_d[j].wait_recv()
            keep = jnp.where(is_core0, k_ref[d], rka[d])[:, None, :]
            for quarter, source in ((x, oe), (1 - x, rd)):
                entry = source[d].astype(f32)
                mine = jnp.where(
                    is_core0, s_ref[c, quarter, d].astype(f32), ra[quarter, d].astype(f32)
                )
                after = keep * entry + mine
                e_s[c, quarter, d] = jnp.where(is_core0, entry, after).astype(bf16)
                se[quarter, d] = jnp.where(is_core0, after, entry).astype(bf16)
            step_e[j].start()
        if j > 0:
            i = j - 1
            step_e[i].wait_recv()
            grown = jnp.exp(cum_ref[i])
            for n in range(size // 2):
                lanes = slice(i * cols + n * 128, i * cols + (n + 1) * 128)
                entry = jnp.concatenate(
                    [
                        e_s[q // 2, q % 2, i * size + h]
                        for h in (2 * n, 2 * n + 1)
                        for q in range(4)
                    ],
                    0,
                )
                carried = jnp.dot(entry, c_cols, preferred_element_type=f32)
                carried = jnp.concatenate(
                    [
                        carried[:P_SIZE] * grown[2 * n : 2 * n + 1],
                        carried[P_SIZE:] * grown[2 * n + 1 : 2 * n + 2],
                    ],
                    0,
                ).T
                gated = (y_s[:, lanes] + carried) * silu(z_s[:, lanes].astype(f32))
                squares = squares + gated * gated
                hid_s[:, lanes] = (gated * gain_ref[lanes][None, :]).astype(bf16)

    sq_own[...] = lax.dot_general(
        jnp.ones((8, 128), f32), squares, (((1,), (1,)), ((), ())),
        precision=lax.Precision.HIGHEST, preferred_element_type=f32,
    )
    if chunks:
        sq_copy = pltpu.make_async_remote_copy(
            src_ref=sq_own, dst_ref=sq_s, send_sem=sq_sem.at[0], recv_sem=sq_sem.at[1],
            device_id=(idx, 1 - hd), device_id_type=MESH,
        )
        sq_copy.start()
        copies = []
        for i in range(2 * chunks):
            loads[i].wait()
            flipped = jnp.dot(hid_s[...], w_s[i], preferred_element_type=f32).T.astype(bf16)
            j = i % chunks
            rows = pl.ds(j * CHUNK, CHUNK)
            if i < chunks:
                send_s[j] = flipped
                cp = pltpu.make_async_remote_copy(
                    src_ref=send_s.at[j], dst_ref=got_s.at[j],
                    send_sem=psend.at[j], recv_sem=precv.at[j],
                    device_id=(idx, 1 - hd), device_id_type=MESH,
                )
                cp.start()
                copies.append(cp)
            else:
                out_ref[rows] = flipped
        sq_copy.wait()
        total = sq_own[0:1] + sq_s[0:1]
        inverse = lax.rsqrt(total / (HEADS * P_SIZE) + EPSILON)
        for j, cp in enumerate(copies):
            cp.wait()
            rows = pl.ds(j * CHUNK, CHUNK)
            both = out_ref[rows].astype(f32) + got_s[j].astype(f32)
            out_ref[rows] = (both * inverse).astype(bf16)

    for cp in across:
        cp.wait_send()

    @pl.when(has_right)
    def _():
        for cp in ahead:
            cp.wait_send()

    ka.wait_send()
    kb.wait_send()
    for j in range(STEPS):
        step_a[j].wait_send()
        step_b[j].wait_send()
        step_d[j].wait_send()
        step_e[j].wait_send()

    @pl.when(has_next)
    def _():
        for cp in step_c:
            cp.wait_send()


def on_device(
    x_in, z_in, bc_in, dt_in, dt_bias, decay_rate, d_skip, conv_x, conv_bc, norm_gain, w_out
):
    length, hid = x_in.shape
    heads = hid // P_SIZE
    states = jax.ShapeDtypeStruct((2, 2, heads, P_SIZE // 4, N), jnp.bfloat16)
    keep = jax.ShapeDtypeStruct((heads, N), jnp.float32)
    count = lax.axis_size("ctx")
    ranks = lax.axis_size("head")
    depth, width = w_out.shape
    paired = ranks == 2 and width % (2 * CHUNK) == 0
    chunks = width // 2 // CHUNK if paired else 0
    quarter = (heads,) + states.shape[3:]
    vmem = pl.BlockSpec(memory_space=pltpu.VMEM)
    bf, f32 = jnp.bfloat16, jnp.float32
    dma = pltpu.SemaphoreType.DMA
    rows8 = (8, length)
    if paired:
        outs = [jax.ShapeDtypeStruct((width // 2, length), bf)]
        scratch = [
            pltpu.VMEM((2 * chunks, depth, CHUNK), bf),
            pltpu.VMEM((chunks, CHUNK, length), bf),
            pltpu.VMEM((chunks, CHUNK, length), bf),
            pltpu.VMEM(rows8, f32),
            pltpu.VMEM(rows8, f32),
            pltpu.VMEM((length, hid), bf),
            dma((2 * chunks,)),
            dma((chunks,)),
            dma((chunks,)),
            dma((2,)),
        ]
    else:
        outs = [jax.ShapeDtypeStruct((length, hid), bf), jax.ShapeDtypeStruct(rows8, f32)]
        scratch = []
    scratch += [
        pltpu.VMEM(states.shape, bf),
        pltpu.VMEM(keep.shape, f32),
        pltpu.VMEM((length, hid), bf),
        pltpu.VMEM((length, length), f32),
        pltpu.VMEM((STEPS,) + rows8, f32),
        pltpu.VMEM((STEPS,) + rows8, f32),
        pltpu.VMEM((N, length), bf),
        pltpu.VMEM((N, length), bf),
        pltpu.VMEM((length, hid), bf),
        pltpu.VMEM((2 * N, length), bf),
        pltpu.VMEM((2 * N, 128), bf),
        pltpu.VMEM((16, hid), bf),
        dma((3, ranks)),
        dma((3, ranks)),
        pltpu.VMEM((length, hid), bf),
        dma((2,)),
        pltpu.VMEM((length, hid), f32),
        pltpu.VMEM(states.shape, bf),
        pltpu.VMEM((2,) + quarter, bf),
        pltpu.VMEM(keep.shape, f32),
        pltpu.VMEM((2,) + quarter, bf),
        pltpu.VMEM(keep.shape, f32),
        pltpu.VMEM(quarter, bf),
        pltpu.VMEM(keep.shape, f32),
    ]
    scratch += [pltpu.VMEM(quarter, bf)] * 5
    scratch += [
        pltpu.VMEM((2,) + quarter, bf),
        dma((5, STEPS)),
        dma((5, STEPS)),
        dma((2,)),
        dma((2,)),
    ]
    result = pl.pallas_call(
        functools.partial(mixer_kernel, count, ranks, chunks),
        out_shape=outs,
        in_specs=[vmem] * 6
        + [pl.BlockSpec(memory_space=pltpu.SMEM), vmem]
        + [pl.BlockSpec(memory_space=pl.ANY)] * 3,
        out_specs=[vmem] * len(outs),
        scratch_shapes=scratch,
        compiler_params=pltpu.CompilerParams(
            collective_id=0, has_side_effects=True, vmem_limit_bytes=60 * 1024 * 1024
        ),
    )(
        bc_in, dt_in, dt_bias, decay_rate, conv_x, conv_bc.T, d_skip, norm_gain,
        x_in, z_in, w_out,
    )
    if not paired:
        return project_any(result[0], result[1], w_out)
    return result[0]


def project_any(hidden, squares, w_out):
    inverse = lax.rsqrt(lax.psum(squares[0], "head") / (HEADS * P_SIZE) + EPSILON)
    ranks = lax.axis_size("head")
    rank = lax.axis_index("head")
    share = w_out.shape[1] // ranks

    def project(owner):
        rows = lax.dynamic_slice_in_dim(w_out, owner * share, share, 1)
        return lax.dot_general(
            rows, hidden, (((0,), (1,)), ((), ())), preferred_element_type=jnp.float32
        ).astype(jnp.bfloat16)

    arrived = []
    for shift in range(1, ranks):
        piece = project(lax.rem(rank + shift, ranks))
        arrived.append(
            lax.ppermute(piece, "head", [(i, (i + shift) % ranks) for i in range(ranks)])
        )
    total = project(rank).astype(jnp.float32)
    for piece in arrived:
        total = total + piece.astype(jnp.float32)
    return (total * inverse[None, :]).astype(jnp.bfloat16)


def solution(mesh):
    in_specs = (
        P("ctx", "head"),
        P("ctx", "head"),
        P("head", "ctx"),
        P("head", "ctx"),
        P("head"),
        P("head"),
        P("head"),
        P(None, "head"),
        P(),
        P("head"),
        P("head", None),
    )
    out_specs = P("head", "ctx")
    return jax.shard_map(
        on_device, mesh=mesh, in_specs=in_specs, out_specs=out_specs, check_vma=False
    )
```
